256 devices in a mesh: dp: 64 (over z, y, core), heads: 4 (over x).
Axes of the slice: x: 4, y: 4, z: 8, core: 2. Of those that a mesh axis runs over, the one named last changes fastest.
Arguments:
- queries: bfloat16 [64, 128, 8192], P('dp', None, 'heads'), may hold values from -24 to 24
- query_gain: float32 [128], replicated, may hold values from 0.5 to 6
- image_key_rows: bfloat16 [128, 1601, 1024], P('dp', None, 'heads'), may hold values from -24 to 24
- image_value_rows: bfloat16 [128, 1601, 1024], P('dp', None, 'heads'), may hold values from -6 to 6
- key_gain: float32 [128], replicated, may hold values from 0.5 to 6
- gate_logit: float32 [1], replicated, may hold values from 0.3 to 1.5
- image_doc: int32 [128], replicated, may hold values from 0 to 63, as said below
- text_mask: int32 [64, 128, 5], replicated, may hold values from 0 to 1, as said below
- out_grad: bfloat16 [64, 128, 8192], P('dp', None, 'heads'), may hold values from -6 to 6
Outputs:
- attended: bfloat16 [64, 128, 8192], P('dp', None, 'heads')
- query_grad: bfloat16 [64, 128, 8192], P('dp', None, 'heads')
- image_key_gradient: bfloat16 [128, 1601, 1024], P('dp', None, 'heads')
- image_value_gradient: bfloat16 [128, 1601, 1024], P('dp', None, 'heads')
- query_gain_grad: float32 [128], replicated
- key_gain_grad: float32 [128], replicated
- gate_grad: float32 [1], replicated
The draws below stay inside these ranges and needn't reach their ends.
Inputs may be any that keep to these rules, and one draw needn't show every extreme that they name: image_doc never falls; each aligned group of 4 documents holds 8 images, every document 1 to 5; in one group the first document has 5 images and the other three 1; where there are 12 documents or more, in another group the last has 5 and the other three 1. text_mask[d, t, k] is 1 when token t of document d sees the document's k-th image; the images of a document stand at rising token positions and a token sees those at or before it; columns from the document's image count on are 0.
All inputs are finite; a program needn't handle non-finite values.
Results may differ from the reference program's by a relative error of at most 0.0075.
The reference program's roundings to bfloat16 on the way count: a program that leaves them out, or rounds other values in their place, can miss the bound.
Values may be sent and summed in bfloat16 or wider, within the bound.
A program may use at most 192 MiB of HBM per device.

```python
import math
import jax
import jax.numpy as jnp
from jax import lax

QUERY_HEAD_COUNT = 64
KEY_VALUE_HEADS = 8
HEAD_SIZE = 128
IMAGE_TOKENS = 1601
MAXIMG = 5
DOCUMENT_TOKENS = 128
DOCS = 64
IMAGE_COUNT = 128


def spread_factor_scale(random_seed_key, complete_shape, lower, upper):
    return jnp.exp(jax.random.uniform(random_seed_key, complete_shape, jnp.float32, math.log(lower), math.log(upper)))


def image_plan(random_seed_key):
    first_key, second_key = jax.random.split(jax.random.fold_in(random_seed_key, 500), 2)
    group_count = DOCS // 4
    chosen = jax.random.permutation(first_key, group_count)
    front_group = chosen[0]
    extra_picks = jax.random.randint(second_key, (group_count, 4), 0, 4)
    member_ids = jnp.arange(4, dtype=jnp.int32)
    drawn_counts = 1 + jnp.sum((extra_picks[:, :, None] == member_ids[None, None, :]).astype(jnp.int32), axis=1)
    group_ids = jnp.arange(group_count, dtype=jnp.int32)[:, None]
    front_counts = jnp.where(member_ids[None, :] == 0, MAXIMG, 1)
    back_counts = jnp.where(member_ids[None, :] == 3, MAXIMG, 1)
    doc_counts = drawn_counts
    if group_count > 2:
        back_group = chosen[1]
        doc_counts = jnp.where(group_ids == back_group, back_counts, doc_counts)
    doc_counts = jnp.where(group_ids == front_group, front_counts, doc_counts).reshape(DOCS)
    count_ends = jnp.cumsum(doc_counts)
    doc_of_image = jnp.sum((count_ends[None, :] <= jnp.arange(IMAGE_COUNT, dtype=jnp.int32)[:, None]).astype(jnp.int32), axis=1)
    return (doc_counts.astype(jnp.int32), doc_of_image.astype(jnp.int32))


def draw_image_doc(key, part):
    doc_counts, doc_of_image = image_plan(key)
    return doc_of_image


def draw_text_mask(key, part):
    doc_counts, doc_of_image = image_plan(key)
    key = jax.random.fold_in(key, 12)
    doc_span = DOCUMENT_TOKENS // doc_counts
    offsets = jax.random.randint(key, (DOCS, MAXIMG), 0, doc_span[:, None])
    image_index = jnp.arange(MAXIMG, dtype=jnp.int32)
    starts = image_index[None, :] * doc_span[:, None] + offsets
    positions = jnp.arange(DOCUMENT_TOKENS, dtype=jnp.int32)
    visible = (positions[None, :, None] >= starts[:, None, :]) & (image_index[None, None, :] < doc_counts[:, None, None])
    return visible.astype(jnp.int32)


def draw_queries(key, part):
    key = jax.random.fold_in(key, 1)
    drawn_key, row_random_key, column_random_key = jax.random.split(key, 3)
    complete_shape = (DOCS, DOCUMENT_TOKENS, QUERY_HEAD_COUNT, HEAD_SIZE)
    row_factor_scale = spread_factor_scale(row_random_key, (DOCS, DOCUMENT_TOKENS, QUERY_HEAD_COUNT, 1), 0.2, 2.0)
    column_factor_scale = spread_factor_scale(column_random_key, (1, 1, QUERY_HEAD_COUNT, HEAD_SIZE), 0.3, 3.0)
    sampled_draw = jnp.clip(jax.random.normal(drawn_key, complete_shape, jnp.float32), -4.0, 4.0) * row_factor_scale * column_factor_scale
    return sampled_draw.reshape(DOCS, DOCUMENT_TOKENS, QUERY_HEAD_COUNT * HEAD_SIZE).astype(jnp.bfloat16)


def draw_image_key_rows(key, part):
    key = jax.random.fold_in(key, 2)
    drawn_key, row_random_key, column_random_key = jax.random.split(key, 3)
    complete_shape = (IMAGE_COUNT, IMAGE_TOKENS, KEY_VALUE_HEADS, HEAD_SIZE)
    row_factor_scale = spread_factor_scale(row_random_key, (IMAGE_COUNT, IMAGE_TOKENS, KEY_VALUE_HEADS, 1), 0.2, 2.0)
    column_factor_scale = spread_factor_scale(column_random_key, (1, 1, KEY_VALUE_HEADS, HEAD_SIZE), 0.3, 3.0)
    sampled_draw = jnp.clip(jax.random.normal(drawn_key, complete_shape, jnp.float32), -4.0, 4.0) * row_factor_scale * column_factor_scale
    return sampled_draw.reshape(IMAGE_COUNT, IMAGE_TOKENS, KEY_VALUE_HEADS * HEAD_SIZE).astype(jnp.bfloat16)


def draw_image_value_rows(key, part):
    key = jax.random.fold_in(key, 3)
    complete_shape = (IMAGE_COUNT, IMAGE_TOKENS, KEY_VALUE_HEADS * HEAD_SIZE)
    image_share = (jnp.arange(IMAGE_COUNT, dtype=jnp.float32) / IMAGE_COUNT)[:, None, None]
    sampled_draw = jnp.clip(jax.random.normal(key, complete_shape, jnp.float32), -4.0, 4.0) * (0.5 + image_share)
    return sampled_draw.astype(jnp.bfloat16)


def draw_out_grad(key, part):
    key = jax.random.fold_in(key, 4)
    drawn_key = jax.random.fold_in(key, 0)
    complete_shape = (DOCS, DOCUMENT_TOKENS, QUERY_HEAD_COUNT * HEAD_SIZE)
    position_share = (jnp.arange(DOCUMENT_TOKENS, dtype=jnp.float32) / DOCUMENT_TOKENS)[None, :, None]
    sampled_draw = jnp.clip(jax.random.normal(drawn_key, complete_shape, jnp.float32), -4.0, 4.0) * (0.5 + position_share)
    return sampled_draw.astype(jnp.bfloat16)


def draw_query_gain(key, part):
    key = jax.random.fold_in(key, 5)
    sampled_draw = 0.5 * jnp.exp(jax.random.uniform(key, (HEAD_SIZE,), jnp.float32, 0.0, math.log(4.0)))
    return sampled_draw


def draw_key_gain(key, part):
    key = jax.random.fold_in(key, 6)
    sampled_draw = 0.5 * jnp.exp(jax.random.uniform(key, (HEAD_SIZE,), jnp.float32, 0.0, math.log(4.0)))
    return sampled_draw


def setup_inputs(seed: int = 0) -> dict:
    key_list = jax.random.split(jax.random.key(seed), 10)
    queries = draw_queries(jax.random.fold_in(key_list[9], 71), 0)
    query_gain = draw_query_gain(jax.random.fold_in(key_list[9], 71), 0)
    image_key_rows = draw_image_key_rows(jax.random.fold_in(key_list[9], 71), 0)
    image_value_rows = draw_image_value_rows(jax.random.fold_in(key_list[9], 71), 0)
    key_gain = draw_key_gain(jax.random.fold_in(key_list[9], 71), 0)
    gate_logit = jnp.clip(jax.random.uniform(key_list[5], (1,), jnp.float32, 0.3, 1.5), 0.3, 1.5)
    image_doc = draw_image_doc(jax.random.fold_in(key_list[9], 71), 0)
    text_mask = draw_text_mask(jax.random.fold_in(key_list[9], 71), 0)
    out_grad = draw_out_grad(jax.random.fold_in(key_list[9], 71), 0)
    return dict(queries=queries, query_gain=query_gain, image_key_rows=image_key_rows, image_value_rows=image_value_rows, key_gain=key_gain, gate_logit=gate_logit, image_doc=image_doc, text_mask=text_mask, out_grad=out_grad)


EPSILON = 1e-05
NEGATIVE = -1e+30
HIGHEST = lax.Precision.HIGHEST

def normalized_rows(tensor):
    widened = tensor.astype(jnp.float32)
    inverse = lax.rsqrt(lax.optimization_barrier(jnp.mean(widened * widened, axis=-1, keepdims=True)) + EPSILON)
    return (widened * inverse, inverse)

def unit_back(upstream, normed, inverse, gain_row):
    scaled = upstream * gain_row
    result_grad = inverse * (scaled - normed * lax.optimization_barrier(jnp.mean(scaled * normed, axis=-1, keepdims=True)))
    return (result_grad, lax.optimization_barrier(jnp.sum((upstream * normed).reshape(-1, normed.shape[-1]), axis=0)))

def image_tables(image_doc, text_mask):
    slot_ids = jnp.arange(IMAGE_COUNT, dtype=jnp.int32)
    same_doc = image_doc[:, None] == image_doc[None, :]
    earlier = slot_ids[None, :] < slot_ids[:, None]
    image_rank = lax.optimization_barrier(jnp.sum((same_doc & earlier).astype(jnp.int32), axis=1))
    rank_hot = (image_rank[:, None] == jnp.arange(MAXIMG, dtype=jnp.int32)[None, :]).astype(jnp.int32)
    seen_rows = lax.optimization_barrier(jnp.sum(text_mask[image_doc] * rank_hot[:, None, :], axis=2)) > 0
    doc_hot = (image_doc[None, :] == jnp.arange(DOCS, dtype=jnp.int32)[:, None]).astype(jnp.float32)
    return (seen_rows, doc_hot)

def reference(queries, query_gain, image_key_rows, image_value_rows, key_gain, gate_logit, image_doc, text_mask, out_grad):
    heads_per_group = QUERY_HEAD_COUNT // KEY_VALUE_HEADS
    score_scale = HEAD_SIZE ** (-0.5)
    query_unit, query_inverse = normalized_rows(queries.reshape(DOCS, DOCUMENT_TOKENS, QUERY_HEAD_COUNT, HEAD_SIZE))
    query_hat = (query_unit * query_gain).astype(jnp.bfloat16)
    key_unit_rows, key_inverse_norm = normalized_rows(image_key_rows.reshape(IMAGE_COUNT, IMAGE_TOKENS, KEY_VALUE_HEADS, HEAD_SIZE))
    key_hat = (key_unit_rows * key_gain).astype(jnp.bfloat16)
    value_matrix = image_value_rows.reshape(IMAGE_COUNT, IMAGE_TOKENS, KEY_VALUE_HEADS, HEAD_SIZE)
    seen_rows, doc_hot = image_tables(image_doc, text_mask)
    gate_tanh = jnp.tanh(gate_logit[0])
    grad_scaled = (gate_tanh * out_grad.astype(jnp.float32)).astype(jnp.bfloat16).reshape(DOCS, DOCUMENT_TOKENS, QUERY_HEAD_COUNT, HEAD_SIZE)

    def image_scores(query_row_matrix, key_rows):
        regrouped = query_row_matrix.reshape(DOCUMENT_TOKENS, KEY_VALUE_HEADS, heads_per_group, HEAD_SIZE).astype(jnp.float32)
        return jnp.einsum('lkgd,ckd->kglc', regrouped, key_rows.astype(jnp.float32), precision=HIGHEST) * score_scale

    def image_forward(inputs):
        key_rows, value_rows, doc_index, seen_image = inputs
        query_row_matrix = lax.dynamic_index_in_dim(query_hat, doc_index, 0, keepdims=False)
        scores = image_scores(query_row_matrix, key_rows)
        row_max = lax.optimization_barrier(jnp.max(scores, axis=-1, keepdims=True))
        log_total = row_max + jnp.log(lax.optimization_barrier(jnp.sum(jnp.exp(scores - row_max), axis=-1, keepdims=True)))
        soft_prob = jnp.exp(scores - log_total).astype(jnp.bfloat16).astype(jnp.float32)
        image_out = jnp.einsum('kglc,ckd->lkgd', soft_prob, value_rows.astype(jnp.float32), precision=HIGHEST)
        image_out = jnp.where(seen_image[:, None, None], image_out.reshape(DOCUMENT_TOKENS, QUERY_HEAD_COUNT, HEAD_SIZE), 0.0)
        image_lse = jnp.transpose(log_total[..., 0], (2, 0, 1)).reshape(DOCUMENT_TOKENS, QUERY_HEAD_COUNT)
        image_lse = jnp.where(seen_image[:, None], image_lse, NEGATIVE)
        return (image_out, image_lse)
    image_outs, image_lses = lax.map(image_forward, (key_hat, value_matrix, image_doc, seen_rows))
    doc_max = lax.optimization_barrier(jnp.max(jnp.where(doc_hot[:, :, None, None] > 0.5, image_lses[None], 2.0 * NEGATIVE), axis=1))
    exp_terms = jnp.exp(image_lses - doc_max[image_doc])
    doc_total = jnp.einsum('di,ilh->dlh', doc_hot, exp_terms, precision=HIGHEST)
    doc_lse = doc_max + jnp.log(doc_total)
    weight = exp_terms / doc_total[image_doc]
    merged = jnp.einsum('di,ilhe->dlhe', doc_hot, weight[..., None] * image_outs, precision=HIGHEST)
    attended = (gate_tanh * merged).astype(jnp.bfloat16).reshape(DOCS, DOCUMENT_TOKENS, QUERY_HEAD_COUNT * HEAD_SIZE)
    row_delta = lax.optimization_barrier(jnp.sum(grad_scaled.astype(jnp.float32) * merged, axis=-1))
    gate_total = jnp.sum(out_grad.astype(jnp.float32).reshape(DOCS, DOCUMENT_TOKENS, QUERY_HEAD_COUNT, HEAD_SIZE) * merged)
    gate_grad = ((1.0 - gate_tanh * gate_tanh) * gate_total).reshape(1)

    def image_backward(inputs):
        key_rows, value_rows, doc_index, seen_image = inputs
        query_row_matrix = lax.dynamic_index_in_dim(query_hat, doc_index, 0, keepdims=False)
        gradient_rows = lax.dynamic_index_in_dim(grad_scaled, doc_index, 0, keepdims=False)
        logsumexp_rows = lax.dynamic_index_in_dim(doc_lse, doc_index, 0, keepdims=False)
        delta_per_row = lax.dynamic_index_in_dim(row_delta, doc_index, 0, keepdims=False)
        scores = image_scores(query_row_matrix, key_rows)
        logsumexp_by_group = jnp.transpose(logsumexp_rows.reshape(DOCUMENT_TOKENS, KEY_VALUE_HEADS, heads_per_group), (1, 2, 0))[..., None]
        delta_by_group = jnp.transpose(delta_per_row.reshape(DOCUMENT_TOKENS, KEY_VALUE_HEADS, heads_per_group), (1, 2, 0))[..., None]
        soft_prob = jnp.where(seen_image[None, None, :, None], jnp.exp(scores - logsumexp_by_group), 0.0)
        gradient_by_group = gradient_rows.reshape(DOCUMENT_TOKENS, KEY_VALUE_HEADS, heads_per_group, HEAD_SIZE).astype(jnp.float32)
        value_part = jnp.einsum('kglc,lkgd->ckd', soft_prob.astype(jnp.bfloat16).astype(jnp.float32), gradient_by_group, precision=HIGHEST)
        prob_grad = jnp.einsum('lkgd,ckd->kglc', gradient_by_group, value_rows.astype(jnp.float32), precision=HIGHEST)
        score_grad = (soft_prob * (prob_grad - delta_by_group)).astype(jnp.bfloat16).astype(jnp.float32)
        query_part = jnp.einsum('kglc,ckd->lkgd', score_grad, key_rows.astype(jnp.float32), precision=HIGHEST) * score_scale
        query_by_group = query_row_matrix.reshape(DOCUMENT_TOKENS, KEY_VALUE_HEADS, heads_per_group, HEAD_SIZE).astype(jnp.float32)
        key_part = jnp.einsum('kglc,lkgd->ckd', score_grad, query_by_group, precision=HIGHEST) * score_scale
        return (query_part.reshape(DOCUMENT_TOKENS, QUERY_HEAD_COUNT, HEAD_SIZE), key_part, value_part)
    query_parts, key_parts, value_pieces = lax.map(image_backward, (key_hat, value_matrix, image_doc, seen_rows))
    hat_grad = jnp.einsum('di,ilhe->dlhe', doc_hot, query_parts, precision=HIGHEST)
    query_back, query_gain_grad = unit_back(hat_grad, query_unit, query_inverse, query_gain)
    key_reverse_pass, key_gain_grad = unit_back(key_parts, key_unit_rows, key_inverse_norm, key_gain)
    query_grad = query_back.astype(jnp.bfloat16).reshape(DOCS, DOCUMENT_TOKENS, QUERY_HEAD_COUNT * HEAD_SIZE)
    image_key_gradient = key_reverse_pass.astype(jnp.bfloat16).reshape(IMAGE_COUNT, IMAGE_TOKENS, KEY_VALUE_HEADS * HEAD_SIZE)
    image_value_gradient = value_pieces.astype(jnp.bfloat16).reshape(IMAGE_COUNT, IMAGE_TOKENS, KEY_VALUE_HEADS * HEAD_SIZE)
    return (attended, query_grad, image_key_gradient, image_value_gradient, query_gain_grad, key_gain_grad, gate_grad)
```

```python
import functools

import jax
import jax.numpy as jnp
from jax import lax
from jax.experimental import pallas as pl
from jax.experimental.pallas import tpu as pltpu
from jax.sharding import PartitionSpec as P

EPSILON = 1e-05
NEGATIVE = -1e30
LOG2E = 1.4426950408889634
MESH = pl.DeviceIdType.MESH
F32 = jnp.float32
BF16 = jnp.bfloat16

GROUP = 4
DIM = 128
TEXT = 128
HEADS = 16
KV = 2
PER = HEADS // KV
CHUNKS = HEADS // 2
ROWS = 2 * TEXT
COLS = 1601
MAIN = 1600
PADDED = 1616
DEEP = 1664
SCALE = DIM ** (-0.5)


def blocks_of(size):
    out = [(a, min(size, MAIN - a)) for a in range(0, MAIN, size)]
    return out + [(MAIN, PADDED - MAIN)]


def dot(a, b):
    return jnp.dot(a, b, preferred_element_type=F32)


def fold(x, op):
    return op(x.reshape(x.shape[0] // 8, 8, x.shape[1]), axis=0)


def main_kernel(
    img_ref,
    gate_ref,
    qgain_ref,
    kgain_ref,
    tm_hbm,
    q_hbm,
    g_hbm,
    k_hbm,
    v_hbm,
    att_hbm,
    dq_hbm,
    dk_hbm,
    dv_hbm,
    part_ref,
    tm_ref,
    qbuf,
    gbuf,
    kraw,
    vraw,
    khat,
    vpad,
    turned,
    qh,
    qhT,
    gs,
    gsT,
    e_ref,
    p_ref,
    ds_ref,
    o_ref,
    dq_ref,
    dk_acc,
    dv_acc,
    m_ref,
    f_ref,
    d_ref,
    w_ref,
    stats,
    own_o,
    near_o,
    far_o,
    own_q,
    near_q,
    far_q,
    rnear_o,
    rfar_o,
    rnear_q,
    rfar_q,
    att_v,
    dq_v,
    load_sem,
    send_sem,
    recv_sem,
    stat_send,
    stat_recv,
    ret_send,
    ret_recv,
    out_sem,
):
    me = lax.axis_index("dp")
    group = me // GROUP
    j = me % GROUP
    base = group * GROUP
    inner = (j == 1) | (j == 2)
    outer = jnp.logical_not(inner)
    near = base + j + 1 - 2 * (j % 2)
    far = base + jnp.where(j < 2, 2, 1)
    far_slot = jnp.where(inner, 2, 3)
    side = jnp.where(j < 2, 0, 1)

    def slot_of(o):
        return o + side - 2 * o * side

    loads = [pltpu.make_async_copy(tm_hbm.at[pl.ds(base, GROUP)], tm_ref, load_sem.at[0])]
    loads.append(pltpu.make_async_copy(q_hbm.at[0], qbuf.at[0], load_sem.at[1]))
    loads.append(pltpu.make_async_copy(g_hbm.at[0], gbuf.at[0], load_sem.at[2]))
    for o in range(2):
        loads.append(pltpu.make_async_copy(k_hbm.at[slot_of(o)], kraw.at[o], load_sem.at[3 + o]))
        loads.append(pltpu.make_async_copy(v_hbm.at[slot_of(o)], vraw.at[o], load_sem.at[5 + o]))
    for c in loads:
        c.start()

    barrier = pltpu.get_barrier_semaphore()
    for step in range(1, GROUP):
        pl.semaphore_signal(
            barrier, inc=1, device_id={"dp": base + (j + step) % GROUP}, device_id_type=MESH
        )
    pl.semaphore_wait(barrier, GROUP - 1)

    def remote(src, dst, ss, rs, dev):
        return pltpu.make_async_remote_copy(
            src_ref=src, dst_ref=dst, send_sem=ss, recv_sem=rs,
            device_id={"dp": dev}, device_id_type=MESH,
        )

    sends = [
        remote(q_hbm.at[0], qbuf.at[1], send_sem.at[0], recv_sem.at[0, 1], near),
        remote(q_hbm.at[0], qbuf.at[far_slot], send_sem.at[1], recv_sem.at[0, far_slot], far),
        remote(g_hbm.at[0], gbuf.at[1], send_sem.at[2], recv_sem.at[1, 1], near),
        remote(g_hbm.at[0], gbuf.at[far_slot], send_sem.at[3], recv_sem.at[1, far_slot], far),
    ]
    for c in sends:
        c.start()

    def arrived(which, buf, slot):
        src = (q_hbm, g_hbm)[which]
        remote(src.at[0], buf.at[slot], send_sem.at[0], recv_sem.at[which, slot], near).wait_recv()

    docs, rels, ranks = [], [], []
    for o in range(2):
        local = 2 * j + slot_of(o)
        doc = img_ref[2 * base + local]
        rank = jnp.int32(0)
        for i in range(2 * GROUP):
            same = (img_ref[2 * base + i] == doc) & (i < local)
            rank = rank + jnp.where(same, 1, 0)
        doc = doc - base
        rel = jnp.where(
            doc == j, 0, jnp.where(doc == near - base, 1, jnp.where(doc == GROUP - 1 - j, 2, 3))
        )
        docs.append(doc)
        rels.append(rel)
        ranks.append(rank)
    gate = jnp.tanh(jnp.broadcast_to(gate_ref[...], (1, DIM)))

    @pl.when(outer)
    def _():
        for r in (2, 3):
            qbuf[r] = jnp.zeros((TEXT, HEADS * DIM), BF16)
            gbuf[r] = jnp.zeros((TEXT, HEADS * DIM), BF16)

    p_ref[PADDED:DEEP] = jnp.zeros((DEEP - PADDED, ROWS), BF16)
    ds_ref[PADDED:DEEP] = jnp.zeros((DEEP - PADDED, ROWS), BF16)

    loads[0].wait()
    seen = []
    lanes8 = lax.broadcasted_iota(jnp.int32, (TEXT, tm_ref.shape[2]), 1)
    for o in range(2):
        col = jnp.zeros((TEXT, 1), F32)
        for d in range(GROUP):
            hit = (lanes8 == ranks[o]) & (docs[o] == d)
            col = col + jnp.sum(jnp.where(hit, tm_ref[d], 0).astype(F32), axis=1, keepdims=True)
        seen.append(jnp.broadcast_to(col, (TEXT, TEXT)).T[0:1])

    tail_row = lax.broadcasted_iota(jnp.int32, (PADDED - MAIN, DIM), 0) == 0

    def unit_of(x):
        inverse = lax.rsqrt(jnp.mean(x * x, axis=1, keepdims=True) + EPSILON)
        return x * inverse, inverse

    def tail_of(ref, o, lanes):
        row = ref[o, MAIN:COLS, lanes].astype(F32)
        return jnp.where(tail_row, jnp.broadcast_to(row, (PADDED - MAIN, DIM)), 0.0)

    for o in range(2):
        loads[3 + 2 * o].wait()
        loads[4 + 2 * o].wait()

    def prep_kv(u, carry):
        o, k = u // KV, u % KV
        lanes = pl.ds(pl.multiple_of(k * DIM, DIM), DIM)
        for a, n in blocks_of(160):
            if a < MAIN:
                x = kraw[o, a : a + n, lanes].astype(F32)
                vpad[o, k, a : a + n, :] = vraw[o, a : a + n, lanes]
            else:
                x = tail_of(kraw, o, lanes)
                vpad[o, k, a : a + n, :] = tail_of(vraw, o, lanes).astype(BF16)
            unit, _ = unit_of(x)
            khat[o, k, a : a + n, :] = (unit * kgain_ref[...]).astype(BF16)
        return carry

    lax.fori_loop(0, 2 * KV, prep_kv, 0)

    def turn(src, o, k):
        for a in range(0, DEEP, DIM):
            if a + DIM <= PADDED:
                x = src[o, k, a : a + DIM, :].astype(F32)
            else:
                x = jnp.concatenate(
                    [src[o, k, a:PADDED, :].astype(F32), jnp.zeros((a + DIM - PADDED, DIM), F32)], axis=0
                )
            turned[:, a : a + DIM] = x.T.astype(BF16)

    def chosen(buf, o, count, lanes):
        x = buf[0, :, lanes].astype(F32)
        for r in range(1, count):
            x = jnp.where(rels[o] == r, buf[r, :, lanes].astype(F32), x)
        return x

    def prep_q(o, count):
        def body(hc, carry):
            x = chosen(qbuf, o, count, pl.ds(pl.multiple_of(hc * ROWS, ROWS), ROWS))
            for h in range(2):
                unit, _ = unit_of(x[:, h * DIM : (h + 1) * DIM])
                hat = unit * qgain_ref[...]
                qh[o, hc, h * TEXT : (h + 1) * TEXT, :] = hat.astype(BF16)
                qhT[o, hc, :, h * TEXT : (h + 1) * TEXT] = hat.T.astype(BF16)
            return carry

        lax.fori_loop(0, CHUNKS, body, 0)

    def prep_g(o, count):
        def body(hc, carry):
            x = chosen(gbuf, o, count, pl.ds(pl.multiple_of(hc * ROWS, ROWS), ROWS))
            for h in range(2):
                g = gate * x[:, h * DIM : (h + 1) * DIM]
                gs[o, hc, h * TEXT : (h + 1) * TEXT, :] = g.astype(BF16)
                gsT[o, hc, :, h * TEXT : (h + 1) * TEXT] = g.T.astype(BF16)
            return carry

        lax.fori_loop(0, CHUNKS, body, 0)

    def put_row(ref, o, hc, row):
        for h in range(2):
            ref[o, pl.ds(2 * hc + h, 1), :] = row[:, h * TEXT : (h + 1) * TEXT]

    def get_row(ref, o, hc):
        return jnp.concatenate([ref[o, pl.ds(2 * hc + h, 1), :] for h in range(2)], axis=1)

    tail_mask = lax.broadcasted_iota(jnp.int32, (PADDED - MAIN, ROWS), 0) == 0

    def forward(o):
        def per_kv(k, carry):
            turn(vpad, o, k)

            def chunk(c, carry):
                hc = k * (PER // 2) + c
                i = o * CHUNKS + hc
                qT = qhT[o, hc]
                top = jnp.full((8, ROWS), -jnp.inf, F32)
                for a, n in blocks_of(400):
                    s = dot(khat[o, k, a : a + n, :], qT)
                    if a == MAIN:
                        s = jnp.where(tail_mask, s, -jnp.inf)
                    e_ref[i, a : a + n, :] = s
                    top = jnp.maximum(top, fold(s, jnp.max))
                top = jnp.max(top, axis=0, keepdims=True)
                total = jnp.zeros((8, ROWS), F32)
                for a, n in blocks_of(80):
                    e = jnp.exp2((e_ref[i, a : a + n, :] - top) * (SCALE * LOG2E))
                    e_ref[i, a : a + n, :] = e
                    total = total + fold(e, jnp.sum)
                total = jnp.sum(total, axis=0, keepdims=True)
                inverse = 1.0 / total
                for a, n in blocks_of(80):
                    p_ref[a : a + n, :] = (e_ref[i, a : a + n, :] * inverse).astype(BF16)
                o_ref[o, hc] = dot(turned[...], p_ref[...])
                put_row(m_ref, o, hc, top * SCALE)
                put_row(w_ref, o, hc, top * SCALE + jnp.log(total))
                return carry

            lax.fori_loop(0, PER // 2, chunk, 0)
            return carry

        lax.fori_loop(0, KV, per_kv, 0)

    loads[1].wait()
    arrived(0, qbuf, 1)

    @pl.when(inner)
    def _():
        arrived(0, qbuf, 2)

    prep_q(0, 3)
    forward(0)

    @pl.when(inner)
    def _():
        arrived(0, qbuf, 3)

    prep_q(1, 4)
    forward(1)

    loads[2].wait()
    arrived(1, gbuf, 1)

    @pl.when(inner)
    def _():
        arrived(1, gbuf, 2)
        arrived(1, gbuf, 3)

    for o in range(2):
        prep_g(o, 3 + o)

        def delta(hc, carry):
            prod = o_ref[o, hc] * gsT[o, hc].astype(F32)
            put_row(d_ref, o, hc, jnp.sum(prod, axis=0, keepdims=True))
            return carry

        lax.fori_loop(0, CHUNKS, delta, 0)
        saw = jnp.broadcast_to(seen[o], (HEADS, TEXT)) > 0.0
        stats[j, slot_of(o), 0] = jnp.where(saw, w_ref[o], NEGATIVE)
        stats[j, slot_of(o), 1] = jnp.where(saw, d_ref[o], 0.0)

    swaps = []
    for step in range(1, GROUP):
        swaps.append(
            remote(
                stats.at[j], stats.at[j], stat_send.at[step - 1], stat_recv.at[j],
                base + (j + step) % GROUP,
            )
        )
    for c in swaps:
        c.start()
    for step in range(1, GROUP):
        other = (j + step) % GROUP
        remote(stats.at[j], stats.at[other], stat_send.at[0], stat_recv.at[other], near).wait_recv()

    for o in range(2):
        mine = [img_ref[2 * base + i] - base == docs[o] for i in range(2 * GROUP)]
        lses = [
            jnp.where(mine[i], stats[i // 2, i % 2, 0], 2.0 * NEGATIVE) for i in range(2 * GROUP)
        ]
        top = functools.reduce(jnp.maximum, lses)
        terms = [jnp.exp(x - top) for x in lses]
        total = functools.reduce(jnp.add, terms)
        weighted = [
            t * jnp.where(mine[i], stats[i // 2, i % 2, 1], 0.0) for i, t in enumerate(terms)
        ]
        saw = jnp.broadcast_to(seen[o], (HEADS, TEXT)) > 0.0
        own = jnp.where(saw, w_ref[o], NEGATIVE)
        d_ref[o] = functools.reduce(jnp.add, weighted) / total
        f_ref[o] = jnp.where(saw, jnp.exp(m_ref[o] - (top + jnp.log(total))), 0.0)
        w_ref[o] = jnp.where(saw, jnp.exp(own - top) / total, 0.0)

    def share(pair, own_b, near_b, far_b, k, lanes):
        def total(r):
            a = jnp.where(rels[0] == r, pair[0], 0.0)
            return a + jnp.where(rels[1] == r, pair[1], 0.0)

        own_b[k, :, lanes] = total(0)
        near_b[k, :, lanes] = total(1)
        far_b[0, k, :, lanes] = total(2).astype(BF16)
        far_b[1, k, :, lanes] = total(3).astype(BF16)

    def returns(which, k, near_b, far_b, rnear_b, rfar_b):
        one = remote(
            near_b.at[k], rnear_b.at[k], ret_send.at[which, k, 0], ret_recv.at[which, k, 0], near
        )
        two = [
            remote(
                far_b.at[r, k], rfar_b.at[k], ret_send.at[which, k, 1 + r],
                ret_recv.at[which, k, 1], base + jnp.where(j == 1, 2 + r, 1 - r),
            )
            for r in range(2)
        ]
        return one, two

    def start_returns(*args):
        one, two = returns(*args)
        one.start()

        @pl.when(inner)
        def _():
            for c in two:
                c.start()

    def finish_sends(*args):
        one, two = returns(*args)
        one.wait_send()

        @pl.when(inner)
        def _():
            for c in two:
                c.wait_send()

    def wait_returns(*args):
        one, two = returns(*args)
        one.wait_recv()
        two[0].wait_recv()

    o_args = (near_o, far_o, rnear_o, rfar_o)
    q_args = (near_q, far_q, rnear_q, rfar_q)

    def give_out(k, carry):
        def body(c, carry):
            hc = k * (PER // 2) + c
            pair = []
            for o in range(2):
                x = o_ref[o, hc] * get_row(w_ref, o, hc)
                pair.append(jnp.concatenate([x[:, :TEXT].T, x[:, TEXT:].T], axis=1))
            share(pair, own_o, near_o, far_o, k, pl.ds(pl.multiple_of(c * ROWS, ROWS), ROWS))
            return carry

        lax.fori_loop(0, PER // 2, body, 0)
        start_returns(0, k, *o_args)
        return carry

    lax.fori_loop(0, KV, give_out, 0)

    def backward(k, kgain_sum):
        lanes = pl.ds(pl.multiple_of(k * DIM, DIM), DIM)

        def per_slot(o, kgain_sum):
            turn(khat, o, k)
            dk_acc[...] = jnp.zeros_like(dk_acc)
            dv_acc[...] = jnp.zeros_like(dv_acc)

            def chunk(c, carry):
                hc = k * (PER // 2) + c
                i = o * CHUNKS + hc
                gT = gsT[o, hc]
                grows = gs[o, hc]
                qrows = qh[o, hc]
                factor = get_row(f_ref, o, hc)
                delta = get_row(d_ref, o, hc)
                for a, n in blocks_of(160):
                    dp = dot(vpad[o, k, a : a + n, :], gT)
                    p = e_ref[i, a : a + n, :] * factor
                    pb = p.astype(BF16)
                    ds = (p * (dp - delta)).astype(BF16)
                    ds_ref[a : a + n, :] = ds
                    dv_acc[a : a + n, :] += dot(pb, grows)
                    dk_acc[a : a + n, :] += dot(ds, qrows)
                x = dot(turned[...], ds_ref[...])
                dq_ref[o, c] = jnp.concatenate([x[:, :TEXT].T, x[:, TEXT:].T], axis=1)
                return carry

            lax.fori_loop(0, PER // 2, chunk, 0)

            for a, n in blocks_of(160):
                last = a == MAIN
                x = tail_of(kraw, o, lanes) if last else kraw[o, a : a + n, lanes].astype(F32)
                up = dk_acc[a : a + n, :] * SCALE
                unit, inverse = unit_of(x)
                scaled = up * kgain_ref[...]
                back = inverse * (scaled - unit * jnp.mean(scaled * unit, axis=1, keepdims=True))
                kgain_sum = kgain_sum + fold(up * unit, jnp.sum)
                value = dv_acc[a : a + n, :]
                if last:
                    back, value, n = back[:1], value[:1], 1
                kraw[o, a : a + n, lanes] = back.astype(BF16)
                vraw[o, a : a + n, lanes] = value.astype(BF16)
            return kgain_sum

        kgain_sum = lax.fori_loop(0, 2, per_slot, kgain_sum)

        def body(c, carry):
            share(
                [dq_ref[0, c], dq_ref[1, c]], own_q, near_q, far_q, k,
                pl.ds(pl.multiple_of(c * ROWS, ROWS), ROWS),
            )
            return carry

        lax.fori_loop(0, PER // 2, body, 0)
        start_returns(1, k, *q_args)
        return kgain_sum

    kgain_sum = lax.fori_loop(0, KV, backward, jnp.zeros((8, DIM), F32))

    outs = []
    for o in range(2):
        outs.append(pltpu.make_async_copy(kraw.at[o], dk_hbm.at[slot_of(o)], out_sem.at[2 * o]))
        outs.append(pltpu.make_async_copy(vraw.at[o], dv_hbm.at[slot_of(o)], out_sem.at[2 * o + 1]))
    for c in outs:
        c.start()

    for k in range(KV):
        wait_returns(0, k, *o_args)

    def attend(k, gate_sum):
        for c in range(PER):
            lanes = slice(c * DIM, (c + 1) * DIM)
            full = pl.ds(pl.multiple_of(k * PER * DIM + c * DIM, DIM), DIM)
            merged = own_o[k, :, lanes] + rnear_o[k, :, lanes] + rfar_o[k, :, lanes].astype(F32)
            att_v[:, full] = (gate * merged).astype(BF16)
            gate_sum = gate_sum + fold(gbuf[0, :, full].astype(F32) * merged, jnp.sum)
        return gate_sum

    gate_sum = lax.fori_loop(0, KV, attend, jnp.zeros((8, DIM), F32))
    out_att = pltpu.make_async_copy(att_v, att_hbm.at[0], out_sem.at[4])
    out_att.start()

    for k in range(KV):
        wait_returns(1, k, *q_args)

    def finish(k, qgain_sum):
        for c in range(PER):
            lanes = slice(c * DIM, (c + 1) * DIM)
            full = pl.ds(pl.multiple_of(k * PER * DIM + c * DIM, DIM), DIM)
            hat = own_q[k, :, lanes] + rnear_q[k, :, lanes] + rfar_q[k, :, lanes].astype(F32)
            hat = hat * SCALE
            unit, inverse = unit_of(qbuf[0, :, full].astype(F32))
            scaled = hat * qgain_ref[...]
            back = inverse * (scaled - unit * jnp.mean(scaled * unit, axis=1, keepdims=True))
            dq_v[:, full] = back.astype(BF16)
            qgain_sum = qgain_sum + fold(hat * unit, jnp.sum)
        return qgain_sum

    qgain_sum = lax.fori_loop(0, KV, finish, jnp.zeros((8, DIM), F32))
    out_dq = pltpu.make_async_copy(dq_v, dq_hbm.at[0], out_sem.at[5])
    out_dq.start()

    row = lax.broadcasted_iota(jnp.int32, (8, DIM), 0)
    gate_total = jnp.sum(jnp.sum(gate_sum, axis=0, keepdims=True), axis=1, keepdims=True)
    part_ref[...] = jnp.where(
        row == 0,
        jnp.sum(qgain_sum, axis=0, keepdims=True),
        jnp.where(
            row == 1,
            jnp.sum(kgain_sum, axis=0, keepdims=True),
            (1.0 - gate * gate) * gate_total,
        ),
    )

    for c in sends:
        c.wait_send()
    for c in swaps:
        c.wait_send()
    for k in range(KV):
        finish_sends(0, k, *o_args)
        finish_sends(1, k, *q_args)
    for c in outs:
        c.wait()
    out_att.wait()
    out_dq.wait()


def run_main(img, gate, qgain, kgain, text_mask, q, g, kk, vv):
    vm = pltpu.VMEM
    dma = pltpu.SemaphoreType.DMA
    half = (KV, TEXT, PER * DIM)
    slots = text_mask.shape[2]
    scratch = [
        vm((GROUP, TEXT, slots), jnp.int32),
        vm((4, TEXT, HEADS * DIM), BF16),
        vm((4, TEXT, HEADS * DIM), BF16),
        vm((2, COLS, KV * DIM), BF16),
        vm((2, COLS, KV * DIM), BF16),
        vm((2, KV, PADDED, DIM), BF16),
        vm((2, KV, PADDED, DIM), BF16),
        vm((DIM, DEEP), BF16),
        vm((2, CHUNKS, ROWS, DIM), BF16),
        vm((2, CHUNKS, DIM, ROWS), BF16),
        vm((2, CHUNKS, ROWS, DIM), BF16),
        vm((2, CHUNKS, DIM, ROWS), BF16),
        vm((2 * CHUNKS, PADDED, ROWS), F32),
        vm((DEEP, ROWS), BF16),
        vm((DEEP, ROWS), BF16),
        vm((2, CHUNKS, DIM, ROWS), F32),
        vm((2, PER // 2, TEXT, ROWS), F32),
        vm((PADDED, DIM), F32),
        vm((PADDED, DIM), F32),
        vm((2, HEADS, TEXT), F32),
        vm((2, HEADS, TEXT), F32),
        vm((2, HEADS, TEXT), F32),
        vm((2, HEADS, TEXT), F32),
        vm((GROUP, 2, 2, HEADS, TEXT), F32),
        vm(half, F32),
        vm(half, F32),
        vm((2,) + half, BF16),
        vm(half, F32),
        vm(half, F32),
        vm((2,) + half, BF16),
        vm(half, F32),
        vm(half, BF16),
        vm(half, F32),
        vm(half, BF16),
        vm((TEXT, HEADS * DIM), BF16),
        vm((TEXT, HEADS * DIM), BF16),
        dma((7,)),
        dma((4,)),
        dma((2, 4)),
        dma((3,)),
        dma((4,)),
        dma((2, KV, 3)),
        dma((2, KV, 2)),
        dma((6,)),
    ]
    hbm = pl.BlockSpec(memory_space=pl.ANY)
    vmem = pl.BlockSpec(memory_space=pltpu.VMEM)
    return pl.pallas_call(
        main_kernel,
        out_shape=(
            jax.ShapeDtypeStruct(q.shape, BF16),
            jax.ShapeDtypeStruct(q.shape, BF16),
            jax.ShapeDtypeStruct(kk.shape, BF16),
            jax.ShapeDtypeStruct(vv.shape, BF16),
            jax.ShapeDtypeStruct((8, DIM), F32),
        ),
        in_specs=[pl.BlockSpec(memory_space=pltpu.SMEM), vmem, vmem, vmem] + [hbm] * 5,
        out_specs=(hbm, hbm, hbm, hbm, vmem),
        scratch_shapes=scratch,
        compiler_params=pltpu.CompilerParams(
            collective_id=0, has_side_effects=True, vmem_limit_bytes=64 * 1024 * 1024
        ),
    )(img, gate, qgain, kgain, text_mask, q, g, kk, vv)


def stages_of(sizes):
    low = min(8, sizes["dp"])
    out = [("dp", 1, low)]
    if sizes["heads"] > 1:
        out.append(("heads", 1, sizes["heads"]))
    if sizes["dp"] > low:
        out.append(("dp", low, sizes["dp"] // low))
    return out


def sum_kernel(stages, part_ref, qg_out, kg_out, gate_out, *scratch):
    bufs, (send_sem, recv_sem) = scratch[: len(stages)], scratch[len(stages) :]

    def place(stage):
        axis, stride, count = stage
        me = lax.axis_index(axis)
        mine = (me // stride) % count
        return axis, stride, count, me, mine, me - mine * stride

    barrier = pltpu.get_barrier_semaphore()
    partners = 0
    for stage in stages:
        axis, stride, count, me, mine, low = place(stage)
        for step in range(1, count):
            other = low + stride * ((mine + step) % count)
            pl.semaphore_signal(barrier, inc=1, device_id={axis: other}, device_id_type=MESH)
            partners += 1
    pl.semaphore_wait(barrier, partners)

    value = part_ref[...]
    for n, stage in enumerate(stages):
        axis, stride, count, me, mine, low = place(stage)
        buf = bufs[n]
        buf[mine] = value
        copies = []
        for step in range(1, count):
            other = low + stride * ((mine + step) % count)
            c = pltpu.make_async_remote_copy(
                src_ref=buf.at[mine], dst_ref=buf.at[mine], send_sem=send_sem.at[n, step],
                recv_sem=recv_sem.at[n, mine], device_id={axis: other}, device_id_type=MESH,
            )
            c.start()
            copies.append(c)
        for step in range(1, count):
            src = (mine + step) % count
            pltpu.make_async_remote_copy(
                src_ref=buf.at[src], dst_ref=buf.at[src], send_sem=send_sem.at[n, step],
                recv_sem=recv_sem.at[n, src], device_id={axis: low + stride * src},
                device_id_type=MESH,
            ).wait_recv()
        value = buf[0]
        for i in range(1, count):
            value = value + buf[i]
        for c in copies:
            c.wait_send()
    qg_out[...] = value[0:1]
    kg_out[...] = value[1:2]
    gate_out[...] = value[2:3, 0:1]


def run_sum(part, sizes):
    stages = stages_of(sizes)
    vmem = pl.BlockSpec(memory_space=pltpu.VMEM)
    most = max(s[2] for s in stages)
    return pl.pallas_call(
        functools.partial(sum_kernel, stages),
        out_shape=(
            jax.ShapeDtypeStruct((1, DIM), F32),
            jax.ShapeDtypeStruct((1, DIM), F32),
            jax.ShapeDtypeStruct((1, 1), F32),
        ),
        in_specs=[vmem],
        out_specs=(vmem, vmem, vmem),
        scratch_shapes=[pltpu.VMEM((s[2], 8, DIM), F32) for s in stages]
        + [pltpu.SemaphoreType.DMA((len(stages), most))] * 2,
        compiler_params=pltpu.CompilerParams(collective_id=1, has_side_effects=True),
    )(part)


def solution(mesh):
    sizes = dict(mesh.shape)

    def per_device(q, qgain, kk, vv, kgain, gate, img, text_mask, g):
        att, dq, dk, dv, part = run_main(
            img, gate.reshape(1, 1), qgain.reshape(1, DIM), kgain.reshape(1, DIM), text_mask,
            q, g, kk, vv,
        )
        qg, kg, gt = run_sum(part, sizes)
        return att, dq, dk, dv, qg.reshape(DIM), kg.reshape(DIM), gt.reshape(1)

    split = P("dp", None, "heads")
    return jax.shard_map(
        per_device,
        mesh=mesh,
        in_specs=(split, P(), split, split, P(), P(), P(), P(), split),
        out_specs=(split, split, split, split, P(), P(), P()),
        check_vma=False,
    )
```

```python
import functools

import jax
import jax.numpy as jnp
from jax import lax
from jax.experimental import pallas as pl
from jax.experimental.pallas import tpu as pltpu
from jax.sharding import PartitionSpec as P

EPSILON = 1e-05
NEGATIVE = -1e30
LOG2E = 1.4426950408889634
MESH = pl.DeviceIdType.MESH
F32 = jnp.float32
BF16 = jnp.bfloat16

GROUP = 4
DIM = 128
TEXT = 128
HEADS = 16
KV = 2
PER = HEADS // KV
CHUNKS = HEADS // 2
ROWS = 2 * TEXT
SPAN = PER * TEXT
COLS = 1601
MAIN = 1600
PADDED = 1616
DEEP = 1664
SCALE = DIM ** (-0.5)


def dot(a, b):
    return jnp.dot(a, b, preferred_element_type=F32)


def fold(x, op):
    return op(x.reshape(x.shape[0] // 8, 8, x.shape[1]), axis=0)


def place(stage):
    axis, stride, count = stage
    me = lax.axis_index(axis)
    mine = (me // stride) % count
    return axis, stride, count, mine, me - mine * stride


def main_kernel(
    stages,
    img_ref,
    gate_ref,
    qgain_ref,
    kgain_ref,
    tm_hbm,
    q_hbm,
    g_hbm,
    k_hbm,
    v_hbm,
    att_hbm,
    dq_hbm,
    dk_hbm,
    dv_hbm,
    qg_out,
    kg_out,
    gate_out,
    tm_ref,
    qbuf,
    gbuf,
    kraw,
    vraw,
    wide_k,
    wide_v,
    khat,
    vpad,
    turned_k,
    turned_v,
    qh,
    qhT,
    gs,
    gsT,
    e_ref,
    o_ref,
    dq_ref,
    x_acc,
    m_ref,
    f_ref,
    d_ref,
    w_ref,
    gam_ref,
    stats,
    own_o,
    near_o,
    far_o,
    own_q,
    near_q,
    far_q,
    rnear_o,
    rfar_o,
    rnear_q,
    rfar_q,
    att_v,
    dq_v,
    load_sem,
    send_sem,
    recv_sem,
    stat_send,
    stat_recv,
    ret_send,
    ret_recv,
    out_sem,
    sum_send,
    sum_recv,
    *sum_bufs,
):
    me = lax.axis_index("dp")
    group = me // GROUP
    j = me % GROUP
    base = group * GROUP
    base8 = pl.multiple_of(me // 8 * 8, 8)
    inner = (j == 1) | (j == 2)
    outer = jnp.logical_not(inner)
    near = base + j + 1 - 2 * (j % 2)
    far = base + jnp.where(j < 2, 2, 1)
    far_slot = jnp.where(inner, 2, 3)
    side = jnp.where(j < 2, 0, 1)

    def slot_of(o):
        return o + side - 2 * o * side

    loads = [pltpu.make_async_copy(tm_hbm.at[:, pl.ds(base8, 8), :], tm_ref, load_sem.at[0])]
    loads.append(pltpu.make_async_copy(q_hbm.at[0], qbuf.at[0], load_sem.at[1]))
    loads.append(pltpu.make_async_copy(g_hbm.at[0], gbuf.at[0], load_sem.at[2]))
    loads.append(pltpu.make_async_copy(k_hbm, kraw, load_sem.at[3]))
    loads.append(pltpu.make_async_copy(v_hbm, vraw, load_sem.at[4]))
    for c in loads:
        c.start()

    barrier = pltpu.get_barrier_semaphore()
    for step in range(1, GROUP):
        pl.semaphore_signal(
            barrier, inc=1, device_id={"dp": base + (j + step) % GROUP}, device_id_type=MESH
        )
    partners = GROUP - 1
    for stage in stages:
        axis, stride, count, mine, low = place(stage)
        for step in range(1, count):
            other = low + stride * ((mine + step) % count)
            pl.semaphore_signal(barrier, inc=1, device_id={axis: other}, device_id_type=MESH)
            partners += 1
    pl.semaphore_wait(barrier, partners)

    def remote(src, dst, ss, rs, dev):
        return pltpu.make_async_remote_copy(
            src_ref=src, dst_ref=dst, send_sem=ss, recv_sem=rs,
            device_id={"dp": dev}, device_id_type=MESH,
        )

    sends = [
        remote(q_hbm.at[0], qbuf.at[1], send_sem.at[0], recv_sem.at[0, 1], near),
        remote(q_hbm.at[0], qbuf.at[far_slot], send_sem.at[1], recv_sem.at[0, far_slot], far),
        remote(g_hbm.at[0], gbuf.at[1], send_sem.at[2], recv_sem.at[1, 1], near),
        remote(g_hbm.at[0], gbuf.at[far_slot], send_sem.at[3], recv_sem.at[1, far_slot], far),
    ]
    sends[0].start()

    @pl.when(inner)
    def _():
        sends[1].start()

    def arrived(which, buf, slot):
        src = (q_hbm, g_hbm)[which]
        remote(src.at[0], buf.at[slot], send_sem.at[0], recv_sem.at[which, slot], near).wait_recv()

    docs, rels, ranks = [], [], []
    for o in range(2):
        local = 2 * j + slot_of(o)
        doc = img_ref[2 * base + local]
        rank = jnp.int32(0)
        for i in range(2 * GROUP):
            same = (img_ref[2 * base + i] == doc) & (i < local)
            rank = rank + jnp.where(same, 1, 0)
        doc = doc - base
        rel = jnp.where(
            doc == j, 0, jnp.where(doc == near - base, 1, jnp.where(doc == GROUP - 1 - j, 2, 3))
        )
        docs.append(doc)
        rels.append(rel)
        ranks.append(rank)
    gate = jnp.tanh(jnp.broadcast_to(gate_ref[...], (1, DIM)))

    @pl.when(outer)
    def _():
        for r in (2, 3):
            qbuf[r] = jnp.zeros((TEXT, HEADS * DIM), BF16)
            gbuf[r] = jnp.zeros((TEXT, HEADS * DIM), BF16)


    loads[0].wait()
    seen = []
    rank_at = lax.broadcasted_iota(jnp.int32, tm_ref.shape, 0)
    doc_at = lax.broadcasted_iota(jnp.int32, tm_ref.shape, 1)
    for o in range(2):
        hit = (rank_at == ranks[o]) & (doc_at == docs[o] + (base - base8))
        row = jnp.sum(jnp.where(hit, tm_ref[...], 0).astype(F32), axis=0)
        seen.append(jnp.sum(row, axis=0, keepdims=True))

    tail_row = lax.broadcasted_iota(jnp.int32, (PADDED - MAIN, DIM), 0) == 0

    def unit_of(x):
        inverse = lax.rsqrt(jnp.mean(x * x, axis=1, keepdims=True) + EPSILON)
        return x * inverse, inverse

    def rows_of(o, k, a, n):
        return pl.ds(4 * a + 2 * k + slot_of(o), n, stride=4)

    def tail_of(ref, o, k):
        row = ref[pl.ds(4 * MAIN + 2 * k + slot_of(o), 1), :]
        return jnp.where(tail_row, jnp.broadcast_to(row, (PADDED - MAIN, DIM)), 0.0)

    def widen(raw, wide):
        rows = raw.reshape(4 * COLS, DIM)

        def body(i, carry):
            at = pl.ds(pl.multiple_of(i * 320, 320), 320)
            wide[at, :] = rows[at, :].astype(F32)
            return carry

        lax.fori_loop(0, 4 * MAIN // 320, body, 0)
        wide[4 * MAIN : 4 * COLS, :] = rows[4 * MAIN : 4 * COLS, :].astype(F32)

    def narrow(wide, raw):
        rows = raw.reshape(4 * COLS, DIM)

        def body(i, carry):
            at = pl.ds(pl.multiple_of(i * 320, 320), 320)
            rows[at, :] = wide[at, :].astype(BF16)
            return carry

        lax.fori_loop(0, 4 * MAIN // 320, body, 0)
        rows[4 * MAIN : 4 * COLS, :] = wide[4 * MAIN : 4 * COLS, :].astype(BF16)

    loads[3].wait()
    widen(kraw, wide_k)
    loads[4].wait()
    widen(vraw, wide_v)

    def prep_kv(u, carry):
        o, k = u // KV, u % KV
        for a in range(0, DEEP, DIM):
            if a + DIM < MAIN:
                x = wide_k[rows_of(o, k, a, DIM), :]
                v = wide_v[rows_of(o, k, a, DIM), :]
                n = DIM
            else:
                n = PADDED - a
                fill = jnp.zeros((DIM - n, DIM), F32)
                x = [wide_k[rows_of(o, k, a, MAIN - a), :], tail_of(wide_k, o, k), fill]
                v = [wide_v[rows_of(o, k, a, MAIN - a), :], tail_of(wide_v, o, k), fill]
                x, v = jnp.concatenate(x, axis=0), jnp.concatenate(v, axis=0)
            unit, _ = unit_of(x)
            hat = unit * kgain_ref[...]
            khat[o, k, a : a + n, :] = hat.astype(BF16)[:n]
            vpad[o, k, a : a + n, :] = v.astype(BF16)[:n]
            turned_k[o, k, :, a : a + DIM] = hat.T.astype(BF16)
            turned_v[o, k, :, a : a + DIM] = v.T.astype(BF16)
        return carry

    lax.fori_loop(0, 2 * KV, prep_kv, 0)

    @pl.when(outer)
    def _():
        sends[1].start()

    sends[2].start()
    sends[1].wait_send()
    sends[3].start()

    def chosen(buf, o, count, lanes):
        x = buf[0, :, lanes].astype(F32)
        for r in range(1, count):
            x = jnp.where(rels[o] == r, buf[r, :, lanes].astype(F32), x)
        return x

    def prep_q(o, count):
        def body(hc, carry):
            x = chosen(qbuf, o, count, pl.ds(pl.multiple_of(hc * ROWS, ROWS), ROWS))
            k, c = hc // (PER // 2), hc % (PER // 2)
            for h in range(2):
                unit, _ = unit_of(x[:, h * DIM : (h + 1) * DIM])
                hat = unit * qgain_ref[...]
                at = pl.ds(pl.multiple_of(c * ROWS + h * TEXT, TEXT), TEXT)
                qh[o, k, at, :] = hat.astype(BF16)
                qhT[o, k, :, at] = hat.T.astype(BF16)
            return carry

        lax.fori_loop(0, CHUNKS, body, 0)

    def put_rows(ref, o, k, row):
        for h in range(PER):
            ref[o, k * PER + h : k * PER + h + 1, :] = row[:, h * TEXT : (h + 1) * TEXT]

    def get_rows(ref, o, k):
        rows = ref[o, pl.ds(pl.multiple_of(k * PER, PER), PER), :]
        return jnp.concatenate([rows[h : h + 1] for h in range(PER)], axis=1)

    tail_mask = lax.broadcasted_iota(jnp.int32, (PADDED - MAIN, SPAN), 0) == 0
    STEP = 160

    def score_step(u, at, n, top):
        o, k = u // KV, u % KV
        s = dot(khat[o, k, at, :], qhT[o, k])
        if n < STEP:
            s = jnp.where(tail_mask, s, -jnp.inf)
        e_ref[u, at, :] = s
        return jnp.maximum(top, fold(s, jnp.max))

    def exp_step(u, at, top, total):
        e = jnp.exp2((e_ref[u, at, :] - top) * (SCALE * LOG2E))
        e_ref[u, at, :] = e
        return total + fold(e, jnp.sum)

    lowest = jnp.full((8, SPAN), -jnp.inf, F32)
    nothing = jnp.zeros((8, SPAN), F32)

    def sweep(now, ahead, top):
        def body(i, carry):
            total, high = carry
            at = pl.ds(pl.multiple_of(i * STEP, STEP), STEP)
            if ahead is not None:
                high = score_step(ahead, at, STEP, high)
            if now is not None:
                total = exp_step(now, at, top, total)
            return total, high

        total, high = lax.fori_loop(0, MAIN // STEP, body, (nothing, lowest))
        at = slice(MAIN, PADDED)
        if ahead is not None:
            high = score_step(ahead, at, PADDED - MAIN, high)
        if now is not None:
            total = exp_step(now, at, top, total)
        return jnp.sum(total, axis=0, keepdims=True), jnp.max(high, axis=0, keepdims=True)

    def weigh(u, top, total):
        o, k = u // KV, u % KV
        inverse = 1.0 / total
        out = None
        for a in range(0, PADDED, 2 * DIM):
            n = min(2 * DIM, PADDED - a)
            p = (e_ref[u, a : a + n, :] * inverse).astype(BF16)
            if n < 2 * DIM:
                p = jnp.concatenate([p, jnp.zeros((DEEP - a - n, SPAN), BF16)], axis=0)
            part = dot(turned_v[o, k, :, a : a + p.shape[0]], p)
            out = part if out is None else out + part
        o_ref[o, k] = out
        put_rows(m_ref, o, k, top * SCALE)
        put_rows(w_ref, o, k, top * SCALE + jnp.log(total))

    loads[1].wait()
    arrived(0, qbuf, 1)

    @pl.when(inner)
    def _():
        arrived(0, qbuf, 2)

    prep_q(0, 3)
    _, top = sweep(None, 0, None)
    total, ahead = sweep(0, 1, top)
    weigh(0, top, total)
    top = ahead

    @pl.when(inner)
    def _():
        arrived(0, qbuf, 3)

    prep_q(1, 4)
    for u in range(1, 2 * KV):
        total, ahead = sweep(u, u + 1 if u + 1 < 2 * KV else None, top)
        weigh(u, top, total)
        top = ahead

    loads[2].wait()
    arrived(1, gbuf, 1)

    @pl.when(inner)
    def _():
        arrived(1, gbuf, 2)
        arrived(1, gbuf, 3)

    for o in range(2):

        def delta(hc, carry):
            x = chosen(gbuf, o, 3 + o, pl.ds(pl.multiple_of(hc * ROWS, ROWS), ROWS))
            k, c = hc // (PER // 2), hc % (PER // 2)
            out = o_ref[o, k, :, pl.ds(pl.multiple_of(c * ROWS, ROWS), ROWS)]
            for h in range(2):
                part = slice(h * TEXT, (h + 1) * TEXT)
                put = pl.ds(pl.multiple_of(c * ROWS + h * TEXT, TEXT), TEXT)
                raw = x[:, part]
                turned_raw = raw.T
                grad = (gate * turned_raw).astype(BF16)
                gs[o, k, put, :] = (gate * raw).astype(BF16)
                gsT[o, k, :, put] = grad
                at = pl.ds(2 * hc + h, 1)
                d_ref[o, at, :] = jnp.sum(out[:, part] * grad.astype(F32), axis=0, keepdims=True)
                gam_ref[o, at, :] = jnp.sum(out[:, part] * turned_raw, axis=0, keepdims=True)
            return carry

        lax.fori_loop(0, CHUNKS, delta, 0)
        saw = jnp.broadcast_to(seen[o], (HEADS, TEXT)) > 0.0
        stats[j, slot_of(o), 0] = jnp.where(saw, w_ref[o], NEGATIVE)
        stats[j, slot_of(o), 1] = jnp.where(saw, d_ref[o], 0.0)

    swaps = []
    for step in range(1, GROUP):
        swaps.append(
            remote(
                stats.at[j], stats.at[j], stat_send.at[step - 1], stat_recv.at[j],
                base + (j + step) % GROUP,
            )
        )
    for c in swaps:
        c.start()
    for step in range(1, GROUP):
        other = (j + step) % GROUP
        remote(stats.at[j], stats.at[other], stat_send.at[0], stat_recv.at[other], near).wait_recv()

    gate_sum = jnp.zeros((HEADS, TEXT), F32)
    for o in range(2):
        mine = [img_ref[2 * base + i] - base == docs[o] for i in range(2 * GROUP)]
        lses = [
            jnp.where(mine[i], stats[i // 2, i % 2, 0], 2.0 * NEGATIVE) for i in range(2 * GROUP)
        ]
        top = functools.reduce(jnp.maximum, lses)
        terms = [jnp.exp(x - top) for x in lses]
        total = functools.reduce(jnp.add, terms)
        weighted = [
            t * jnp.where(mine[i], stats[i // 2, i % 2, 1], 0.0) for i, t in enumerate(terms)
        ]
        saw = jnp.broadcast_to(seen[o], (HEADS, TEXT)) > 0.0
        own = jnp.where(saw, w_ref[o], NEGATIVE)
        d_ref[o] = functools.reduce(jnp.add, weighted) / total
        f_ref[o] = jnp.where(saw, jnp.exp(m_ref[o] - (top + jnp.log(total))), 0.0)
        w_ref[o] = jnp.where(saw, jnp.exp(own - top) / total, 0.0)
        gate_sum = gate_sum + w_ref[o] * gam_ref[o]

    def share(pair, own_b, near_b, far_b, k, lanes):
        def total(r):
            a = jnp.where(rels[0] == r, pair[0], 0.0)
            return a + jnp.where(rels[1] == r, pair[1], 0.0)

        own_b[k, :, lanes] = total(0)
        near_b[k, :, lanes] = total(1)
        far_b[0, k, :, lanes] = total(2).astype(BF16)
        far_b[1, k, :, lanes] = total(3).astype(BF16)

    def returns(which, k, near_b, far_b, rnear_b, rfar_b):
        one = remote(
            near_b.at[k], rnear_b.at[k], ret_send.at[which, k, 0], ret_recv.at[which, k, 0], near
        )
        two = [
            remote(
                far_b.at[r, k], rfar_b.at[k], ret_send.at[which, k, 1 + r],
                ret_recv.at[which, k, 1], base + jnp.where(j == 1, 2 + r, 1 - r),
            )
            for r in range(2)
        ]
        return one, two

    def start_returns(*args):
        one, two = returns(*args)
        one.start()

        @pl.when(inner)
        def _():
            for c in two:
                c.start()

    def finish_sends(*args):
        one, two = returns(*args)
        one.wait_send()

        @pl.when(inner)
        def _():
            for c in two:
                c.wait_send()

    def wait_returns(*args):
        one, two = returns(*args)
        one.wait_recv()
        two[0].wait_recv()

    o_args = (near_o, far_o, rnear_o, rfar_o)
    q_args = (near_q, far_q, rnear_q, rfar_q)

    def give_out(k, carry):
        def body(c, carry):
            hc = k * (PER // 2) + c
            pair = []
            for o in range(2):
                w = [w_ref[o, pl.ds(2 * hc + h, 1), :] for h in range(2)]
                x = o_ref[o, k, :, pl.ds(pl.multiple_of(c * ROWS, ROWS), ROWS)]
                x = x * jnp.concatenate(w, axis=1)
                pair.append(jnp.concatenate([x[:, :TEXT].T, x[:, TEXT:].T], axis=1))
            share(pair, own_o, near_o, far_o, k, pl.ds(pl.multiple_of(c * ROWS, ROWS), ROWS))
            return carry

        lax.fori_loop(0, PER // 2, body, 0)
        start_returns(0, k, *o_args)
        return carry

    lax.fori_loop(0, KV, give_out, 0)

    def backward(k, sums):
        kgain_sum, qgain_sum = sums

        def per_slot(o, kgain_sum):
            factor = get_rows(f_ref, o, k)
            delta = get_rows(d_ref, o, k)
            for a in range(0, PADDED, 2 * DIM):
                n = min(2 * DIM, PADDED - a)
                dp = dot(vpad[o, k, a : a + n, :], gsT[o, k])
                p = e_ref[2 * o + k, a : a + n, :] * factor
                ds = (p * (dp - delta)).astype(BF16)
                value = dot(p.astype(BF16), gs[o, k])
                up = dot(ds, qh[o, k]) * SCALE
                if n < 2 * DIM:
                    ds = jnp.concatenate([ds, jnp.zeros((DEEP - a - n, SPAN), BF16)], axis=0)
                part = dot(turned_k[o, k, :, a : a + ds.shape[0]], ds)
                if a == 0:
                    x_acc[...] = part
                else:
                    x_acc[...] += part
                whole = min(n, MAIN - a)
                x = wide_k[rows_of(o, k, a, whole), :]
                if whole < n:
                    x = jnp.concatenate([x, tail_of(wide_k, o, k)], axis=0)
                unit, inverse = unit_of(x)
                scaled = up * kgain_ref[...]
                back = inverse * (scaled - unit * jnp.mean(scaled * unit, axis=1, keepdims=True))
                kgain_sum = kgain_sum + fold(up * unit, jnp.sum)
                wide_k[rows_of(o, k, a, whole), :] = back[:whole]
                wide_v[rows_of(o, k, a, whole), :] = value[:whole]
                if whole < n:
                    at = pl.ds(4 * MAIN + 2 * k + slot_of(o), 1)
                    wide_k[at, :] = back[whole : whole + 1]
                    wide_v[at, :] = value[whole : whole + 1]
            for c in range(PER // 2):
                dq_ref[o, c] = jnp.concatenate(
                    [x_acc[:, c * ROWS + h * TEXT : c * ROWS + (h + 1) * TEXT].T for h in range(2)], axis=1
                )
            return kgain_sum

        kgain_sum = lax.fori_loop(0, 2, per_slot, kgain_sum)

        def body(c, qgain_sum):
            pair = [dq_ref[0, c], dq_ref[1, c]]
            share(pair, own_q, near_q, far_q, k, pl.ds(pl.multiple_of(c * ROWS, ROWS), ROWS))
            full = pl.ds(pl.multiple_of(k * PER * DIM + c * ROWS, ROWS), ROWS)
            for o in range(2):
                x = chosen(qbuf, o, 3 + o, full)
                for h in range(2):
                    part = slice(h * DIM, (h + 1) * DIM)
                    unit, _ = unit_of(x[:, part])
                    qgain_sum = qgain_sum + fold(pair[o][:, part] * unit, jnp.sum)
            return qgain_sum

        qgain_sum = lax.fori_loop(0, PER // 2, body, qgain_sum)
        start_returns(1, k, *q_args)
        return kgain_sum, qgain_sum

    zero = jnp.zeros((8, DIM), F32)
    kgain_sum, qgain_sum = lax.fori_loop(0, KV, backward, (zero, zero))

    row = lax.broadcasted_iota(jnp.int32, (8, DIM), 0)
    gate_total = jnp.sum(jnp.sum(gate_sum, axis=0, keepdims=True), axis=1, keepdims=True)
    part = jnp.where(
        row == 0,
        jnp.sum(qgain_sum, axis=0, keepdims=True) * SCALE,
        jnp.where(
            row == 1,
            jnp.sum(kgain_sum, axis=0, keepdims=True),
            (1.0 - gate * gate) * gate_total,
        ),
    )

    def stage_copies(n):
        axis, stride, count, mine, low = place(stages[n])
        buf = sum_bufs[n]
        out, come = [], []
        for step in range(1, count):
            other = (mine + step) % count
            for at, to, found in ((mine, out, step), (other, come, 0)):
                to.append(
                    pltpu.make_async_remote_copy(
                        src_ref=buf.at[at], dst_ref=buf.at[at], send_sem=sum_send.at[n, found],
                        recv_sem=sum_recv.at[n, at], device_id={axis: low + stride * other},
                        device_id_type=MESH,
                    )
                )
        return out, come

    def stage_start(n, value):
        sum_bufs[n][place(stages[n])[3]] = value
        for c in stage_copies(n)[0]:
            c.start()

    def stage_end(n):
        for c in stage_copies(n)[1]:
            c.wait_recv()
        value = sum_bufs[n][0]
        for i in range(1, stages[n][2]):
            value = value + sum_bufs[n][i]
        return value

    stage_start(0, part)

    narrow(wide_k, kraw)
    narrow(wide_v, vraw)
    outs = [
        pltpu.make_async_copy(kraw, dk_hbm, out_sem.at[0]),
        pltpu.make_async_copy(vraw, dv_hbm, out_sem.at[1]),
    ]
    for c in outs:
        c.start()
    part = stage_end(0)
    if len(stages) > 1:
        stage_start(1, part)

    for k in range(KV):
        wait_returns(0, k, *o_args)

    def attend(k, carry):
        for c in range(PER):
            lanes = slice(c * DIM, (c + 1) * DIM)
            full = pl.ds(pl.multiple_of(k * PER * DIM + c * DIM, DIM), DIM)
            merged = own_o[k, :, lanes] + rnear_o[k, :, lanes] + rfar_o[k, :, lanes].astype(F32)
            att_v[:, full] = (gate * merged).astype(BF16)
        return carry

    lax.fori_loop(0, KV, attend, 0)
    out_att = pltpu.make_async_copy(att_v, att_hbm.at[0], out_sem.at[4])
    out_att.start()
    if len(stages) > 1:
        part = stage_end(1)
    if len(stages) > 2:
        stage_start(2, part)

    for k in range(KV):
        wait_returns(1, k, *q_args)

    def finish(k, carry):
        for c in range(PER):
            lanes = slice(c * DIM, (c + 1) * DIM)
            full = pl.ds(pl.multiple_of(k * PER * DIM + c * DIM, DIM), DIM)
            hat = own_q[k, :, lanes] + rnear_q[k, :, lanes] + rfar_q[k, :, lanes].astype(F32)
            hat = hat * SCALE
            unit, inverse = unit_of(qbuf[0, :, full].astype(F32))
            scaled = hat * qgain_ref[...]
            back = inverse * (scaled - unit * jnp.mean(scaled * unit, axis=1, keepdims=True))
            dq_v[:, full] = back.astype(BF16)
        return carry

    lax.fori_loop(0, KV, finish, 0)
    out_dq = pltpu.make_async_copy(dq_v, dq_hbm.at[0], out_sem.at[5])
    out_dq.start()

    if len(stages) > 2:
        part = stage_end(2)
    qg_out[...] = part[0:1]
    kg_out[...] = part[1:2]
    gate_out[...] = part[2:3, 0:1]
    for n in range(len(stages)):
        for c in stage_copies(n)[0]:
            c.wait_send()
    for c in (sends[0], sends[2], sends[3]):
        c.wait_send()
    for c in swaps:
        c.wait_send()
    for k in range(KV):
        finish_sends(0, k, *o_args)
        finish_sends(1, k, *q_args)
    for c in outs:
        c.wait()
    out_att.wait()
    out_dq.wait()


def run_main(stages, img, gate, qgain, kgain, text_mask, q, g, kk, vv):
    vm = pltpu.VMEM
    dma = pltpu.SemaphoreType.DMA
    half = (KV, TEXT, PER * DIM)
    slots = text_mask.shape[0]
    scratch = [
        vm((slots, 8, TEXT), jnp.int32),
        vm((4, TEXT, HEADS * DIM), BF16),
        vm((4, TEXT, HEADS * DIM), BF16),
        vm((COLS, 4, DIM), BF16),
        vm((COLS, 4, DIM), BF16),
        vm((4 * PADDED, DIM), F32),
        vm((4 * PADDED, DIM), F32),
        vm((2, KV, PADDED, DIM), BF16),
        vm((2, KV, PADDED, DIM), BF16),
        vm((2, KV, DIM, DEEP), BF16),
        vm((2, KV, DIM, DEEP), BF16),
        vm((2, KV, SPAN, DIM), BF16),
        vm((2, KV, DIM, SPAN), BF16),
        vm((2, KV, SPAN, DIM), BF16),
        vm((2, KV, DIM, SPAN), BF16),
        vm((2 * KV, PADDED, SPAN), F32),
        vm((2, KV, DIM, SPAN), F32),
        vm((2, PER // 2, TEXT, ROWS), F32),
        vm((DIM, SPAN), F32),
        vm((2, HEADS, TEXT), F32),
        vm((2, HEADS, TEXT), F32),
        vm((2, HEADS, TEXT), F32),
        vm((2, HEADS, TEXT), F32),
        vm((2, HEADS, TEXT), F32),
        vm((GROUP, 2, 2, HEADS, TEXT), F32),
        vm(half, F32),
        vm(half, F32),
        vm((2,) + half, BF16),
        vm(half, F32),
        vm(half, F32),
        vm((2,) + half, BF16),
        vm(half, F32),
        vm(half, BF16),
        vm(half, F32),
        vm(half, BF16),
        vm((TEXT, HEADS * DIM), BF16),
        vm((TEXT, HEADS * DIM), BF16),
        dma((7,)),
        dma((4,)),
        dma((2, 4)),
        dma((3,)),
        dma((4,)),
        dma((2, KV, 3)),
        dma((2, KV, 2)),
        dma((6,)),
        dma((len(stages), max(s[2] for s in stages))),
        dma((len(stages), max(s[2] for s in stages))),
    ] + [vm((s[2], 8, DIM), F32) for s in stages]
    hbm = pl.BlockSpec(memory_space=pl.ANY)
    vmem = pl.BlockSpec(memory_space=pltpu.VMEM)
    return pl.pallas_call(
        functools.partial(main_kernel, stages),
        out_shape=(
            jax.ShapeDtypeStruct(q.shape, BF16),
            jax.ShapeDtypeStruct(q.shape, BF16),
            jax.ShapeDtypeStruct(kk.shape, BF16),
            jax.ShapeDtypeStruct(vv.shape, BF16),
            jax.ShapeDtypeStruct((1, DIM), F32),
            jax.ShapeDtypeStruct((1, DIM), F32),
            jax.ShapeDtypeStruct((1, 1), F32),
        ),
        in_specs=[pl.BlockSpec(memory_space=pltpu.SMEM), vmem, vmem, vmem] + [hbm] * 5,
        out_specs=(hbm, hbm, hbm, hbm, vmem, vmem, vmem),
        scratch_shapes=scratch,
        compiler_params=pltpu.CompilerParams(
            collective_id=0, has_side_effects=True, vmem_limit_bytes=64 * 1024 * 1024
        ),
    )(img, gate, qgain, kgain, text_mask, q, g, kk, vv)


def stages_of(sizes):
    low = min(8, sizes["dp"])
    out = [("dp", 1, low)]
    if sizes["heads"] > 1:
        out.append(("heads", 1, sizes["heads"]))
    if sizes["dp"] > low:
        out.append(("dp", low, sizes["dp"] // low))
    return out


def interleaved(x):
    x = x.transpose(1, 0, 2).reshape(COLS, 2, KV, DIM)
    return x.transpose(0, 2, 1, 3).reshape(COLS, 2 * KV, DIM)


def separated(x):
    return x.reshape(COLS, KV, 2, DIM).transpose(2, 0, 1, 3).reshape(2, COLS, KV * DIM)


def solution(mesh):
    sizes = dict(mesh.shape)

    def per_device(q, qgain, kk, vv, kgain, gate, img, text_mask, g):
        att, dq, dk, dv, qg, kg, gt = run_main(
            stages_of(sizes), img, gate.reshape(1, 1), qgain.reshape(1, DIM),
            kgain.reshape(1, DIM), text_mask.transpose(2, 0, 1), q, g, interleaved(kk),
            interleaved(vv),
        )
        return (
            att, dq, separated(dk), separated(dv), qg.reshape(DIM), kg.reshape(DIM), gt.reshape(1)
        )

    split = P("dp", None, "heads")
    return jax.shard_map(
        per_device,
        mesh=mesh,
        in_specs=(split, P(), split, split, P(), P(), P(), P(), split),
        out_specs=(split, split, split, split, P(), P(), P()),
        check_vma=False,
    )
```

```python
import functools

import jax
import jax.numpy as jnp
from jax import lax
from jax.experimental import pallas as pl
from jax.experimental.pallas import tpu as pltpu
from jax.sharding import PartitionSpec as P

EPSILON = 1e-05
NEGATIVE = -1e30
LOG2E = 1.4426950408889634
MESH = pl.DeviceIdType.MESH
F32 = jnp.float32
BF16 = jnp.bfloat16

GROUP = 4
DIM = 128
TEXT = 128
HEADS = 16
KV = 2
PER = HEADS // KV
CHUNKS = HEADS // 2
ROWS = 2 * TEXT
SPAN = PER * TEXT
COLS = 1601
MAIN = 1600
PADDED = 1616
DEEP = 1664
SCALE = DIM ** (-0.5)


def dot(a, b):
    return jnp.dot(a, b, preferred_element_type=F32)


def fold(x, op):
    return op(x.reshape(x.shape[0] // 8, 8, x.shape[1]), axis=0)


def place(stage):
    axis, stride, count = stage
    me = lax.axis_index(axis)
    mine = (me // stride) % count
    return axis, stride, count, mine, me - mine * stride


def main_kernel(
    stages,
    img_ref,
    gate_ref,
    qgain_ref,
    kgain_ref,
    tm_hbm,
    q_hbm,
    g_hbm,
    k_hbm,
    v_hbm,
    att_hbm,
    dq_hbm,
    dk_hbm,
    dv_hbm,
    qg_out,
    kg_out,
    gate_out,
    tm_ref,
    qbuf,
    gbuf,
    kraw,
    vraw,
    wide_k,
    wide_v,
    khat,
    vpad,
    turned_k,
    turned_v,
    qh,
    qhT,
    gs,
    gsT,
    e_ref,
    o_ref,
    dq_ref,
    x_acc,
    m_ref,
    f_ref,
    d_ref,
    w_ref,
    gam_ref,
    stats,
    own_o,
    near_o,
    far_o,
    own_q,
    near_q,
    far_q,
    rnear_o,
    rfar_o,
    rnear_q,
    rfar_q,
    load_sem,
    send_sem,
    recv_sem,
    stat_send,
    stat_recv,
    ret_send,
    ret_recv,
    out_sem,
    sum_send,
    sum_recv,
    *sum_bufs,
):
    me = lax.axis_index("dp")
    group = me // GROUP
    j = me % GROUP
    base = group * GROUP
    base8 = pl.multiple_of(me // 8 * 8, 8)
    inner = (j == 1) | (j == 2)
    outer = jnp.logical_not(inner)
    near = base + j + 1 - 2 * (j % 2)
    far = base + jnp.where(j < 2, 2, 1)
    far_slot = jnp.where(inner, 2, 3)
    side = jnp.where(j < 2, 0, 1)

    def slot_of(o):
        return o + side - 2 * o * side

    loads = [pltpu.make_async_copy(tm_hbm.at[:, pl.ds(base8, 8), :], tm_ref, load_sem.at[0])]
    loads.append(pltpu.make_async_copy(q_hbm.at[0], qbuf.at[0], load_sem.at[1]))
    loads.append(pltpu.make_async_copy(g_hbm.at[0], gbuf.at[0], load_sem.at[2]))
    loads.append(pltpu.make_async_copy(k_hbm, kraw, load_sem.at[3]))
    loads.append(pltpu.make_async_copy(v_hbm, vraw, load_sem.at[4]))
    for c in loads:
        c.start()

    barrier = pltpu.get_barrier_semaphore()
    for step in range(1, GROUP):
        pl.semaphore_signal(
            barrier, inc=1, device_id={"dp": base + (j + step) % GROUP}, device_id_type=MESH
        )
    partners = GROUP - 1
    for stage in stages:
        axis, stride, count, mine, low = place(stage)
        for step in range(1, count):
            other = low + stride * ((mine + step) % count)
            pl.semaphore_signal(barrier, inc=1, device_id={axis: other}, device_id_type=MESH)
            partners += 1
    pl.semaphore_wait(barrier, partners)

    def remote(src, dst, ss, rs, dev):
        return pltpu.make_async_remote_copy(
            src_ref=src, dst_ref=dst, send_sem=ss, recv_sem=rs,
            device_id={"dp": dev}, device_id_type=MESH,
        )

    def half_of(ref, k):
        return ref.at[:, pl.ds(k * PER * DIM, PER * DIM)]

    def q_send(slot, k, ss, dev):
        return remote(
            half_of(q_hbm.at[0], k), half_of(qbuf.at[slot], k), ss, recv_sem.at[k, slot], dev
        )

    def g_send(slot, ss, dev):
        return remote(g_hbm.at[0], gbuf.at[slot], ss, recv_sem.at[2, slot], dev)

    q_near = [q_send(1, k, send_sem.at[k], near) for k in range(KV)]
    q_far = [q_send(far_slot, k, send_sem.at[2 + k], far) for k in range(KV)]
    g_near = g_send(1, send_sem.at[4], near)
    g_far = g_send(far_slot, send_sem.at[5], far)

    def start_where(condition, *copies):
        @pl.when(condition)
        def _():
            for c in copies:
                c.start()

    q_near[0].start()
    start_where(inner, q_far[0])

    def q_arrived(slot, k):
        q_send(slot, k, send_sem.at[0], near).wait_recv()

    def g_arrived(slot):
        g_send(slot, send_sem.at[0], near).wait_recv()

    docs, rels, ranks = [], [], []
    for o in range(2):
        local = 2 * j + slot_of(o)
        doc = img_ref[2 * base + local]
        rank = jnp.int32(0)
        for i in range(2 * GROUP):
            same = (img_ref[2 * base + i] == doc) & (i < local)
            rank = rank + jnp.where(same, 1, 0)
        doc = doc - base
        rel = jnp.where(
            doc == j, 0, jnp.where(doc == near - base, 1, jnp.where(doc == GROUP - 1 - j, 2, 3))
        )
        docs.append(doc)
        rels.append(rel)
        ranks.append(rank)
    gate = jnp.tanh(jnp.broadcast_to(gate_ref[...], (1, DIM)))

    @pl.when(outer)
    def _():
        for r in (2, 3):
            qbuf[r] = jnp.zeros((TEXT, HEADS * DIM), BF16)
            gbuf[r] = jnp.zeros((TEXT, HEADS * DIM), BF16)


    loads[0].wait()
    seen = []
    rank_at = lax.broadcasted_iota(jnp.int32, tm_ref.shape, 0)
    doc_at = lax.broadcasted_iota(jnp.int32, tm_ref.shape, 1)
    for o in range(2):
        hit = (rank_at == ranks[o]) & (doc_at == docs[o] + (base - base8))
        row = jnp.sum(jnp.where(hit, tm_ref[...], 0).astype(F32), axis=0)
        seen.append(jnp.sum(row, axis=0, keepdims=True))

    tail_row = lax.broadcasted_iota(jnp.int32, (PADDED - MAIN, DIM), 0) == 0

    def unit_of(x):
        inverse = lax.rsqrt(jnp.mean(x * x, axis=1, keepdims=True) + EPSILON)
        return x * inverse, inverse

    def rows_of(o, k, a, n):
        return pl.ds(4 * a + 2 * k + slot_of(o), n, stride=4)

    def tail_of(ref, o, k):
        row = ref[pl.ds(4 * MAIN + 2 * k + slot_of(o), 1), :]
        return jnp.where(tail_row, jnp.broadcast_to(row, (PADDED - MAIN, DIM)), 0.0)

    def widen(raw, wide):
        rows = raw.reshape(4 * COLS, DIM)

        def body(i, carry):
            at = pl.ds(pl.multiple_of(i * 320, 320), 320)
            wide[at, :] = rows[at, :].astype(F32)
            return carry

        lax.fori_loop(0, 4 * MAIN // 320, body, 0)
        wide[4 * MAIN : 4 * COLS, :] = rows[4 * MAIN : 4 * COLS, :].astype(F32)

    def narrow(wide, raw):
        rows = raw.reshape(4 * COLS, DIM)

        def body(i, carry):
            at = pl.ds(pl.multiple_of(i * 320, 320), 320)
            rows[at, :] = wide[at, :].astype(BF16)
            return carry

        lax.fori_loop(0, 4 * MAIN // 320, body, 0)
        rows[4 * MAIN : 4 * COLS, :] = wide[4 * MAIN : 4 * COLS, :].astype(BF16)

    loads[3].wait()
    widen(kraw, wide_k)

    q_near[1].start()
    start_where(inner, q_far[1])
    loads[4].wait()
    widen(vraw, wide_v)

    def prep_kv(u, carry):
        o, k = u // KV, u % KV
        for a in range(0, DEEP, DIM):
            if a + DIM < MAIN:
                x = wide_k[rows_of(o, k, a, DIM), :]
                v = wide_v[rows_of(o, k, a, DIM), :]
                n = DIM
            else:
                n = PADDED - a
                fill = jnp.zeros((DIM - n, DIM), F32)
                x = [wide_k[rows_of(o, k, a, MAIN - a), :], tail_of(wide_k, o, k), fill]
                v = [wide_v[rows_of(o, k, a, MAIN - a), :], tail_of(wide_v, o, k), fill]
                x, v = jnp.concatenate(x, axis=0), jnp.concatenate(v, axis=0)
            unit, _ = unit_of(x)
            hat = unit * kgain_ref[...]
            khat[o, k, a : a + n, :] = hat.astype(BF16)[:n]
            vpad[o, k, a : a + n, :] = v.astype(BF16)[:n]
            turned_k[o, k, :, a : a + DIM] = hat.T.astype(BF16)
            turned_v[o, k, :, a : a + DIM] = v.T.astype(BF16)
        return carry

    lax.fori_loop(0, 2 * KV, prep_kv, 0)

    start_where(outer, q_far[0])
    g_near.start()

    def chosen(buf, o, count, lanes):
        x = buf[0, :, lanes].astype(F32)
        for r in range(1, count):
            x = jnp.where(rels[o] == r, buf[r, :, lanes].astype(F32), x)
        return x

    def prep_q(o, k, count):
        def body(c, carry):
            hc = k * (PER // 2) + c
            x = chosen(qbuf, o, count, pl.ds(pl.multiple_of(hc * ROWS, ROWS), ROWS))
            for h in range(2):
                unit, _ = unit_of(x[:, h * DIM : (h + 1) * DIM])
                hat = unit * qgain_ref[...]
                at = pl.ds(pl.multiple_of(c * ROWS + h * TEXT, TEXT), TEXT)
                qh[o, k, at, :] = hat.astype(BF16)
                qhT[o, k, :, at] = hat.T.astype(BF16)
            return carry

        lax.fori_loop(0, PER // 2, body, 0)

    def put_rows(ref, o, k, row):
        for h in range(PER):
            ref[o, k * PER + h : k * PER + h + 1, :] = row[:, h * TEXT : (h + 1) * TEXT]

    def get_rows(ref, o, k):
        rows = ref[o, pl.ds(pl.multiple_of(k * PER, PER), PER), :]
        return jnp.concatenate([rows[h : h + 1] for h in range(PER)], axis=1)

    tail_mask = lax.broadcasted_iota(jnp.int32, (PADDED - MAIN, SPAN), 0) == 0
    STEP = 400

    def score_step(u, at, n, top):
        o, k = u // KV, u % KV
        s = dot(khat[o, k, at, :], qhT[o, k])
        if n < STEP:
            s = jnp.where(tail_mask, s, -jnp.inf)
        e_ref[u, at, :] = s
        return jnp.maximum(top, fold(s, jnp.max))

    def exp_step(u, at, top, total):
        e = jnp.exp2((e_ref[u, at, :] - top) * (SCALE * LOG2E))
        e_ref[u, at, :] = e
        return total + fold(e, jnp.sum)

    lowest = jnp.full((8, SPAN), -jnp.inf, F32)
    nothing = jnp.zeros((8, SPAN), F32)

    def sweep(now, ahead, top):
        def body(i, carry):
            total, high = carry
            at = pl.ds(pl.multiple_of(i * STEP, STEP), STEP)
            if ahead is not None:
                high = score_step(ahead, at, STEP, high)
            if now is not None:
                total = exp_step(now, at, top, total)
            return total, high

        total, high = lax.fori_loop(0, MAIN // STEP, body, (nothing, lowest))
        at = slice(MAIN, PADDED)
        if ahead is not None:
            high = score_step(ahead, at, PADDED - MAIN, high)
        if now is not None:
            total = exp_step(now, at, top, total)
        return jnp.sum(total, axis=0, keepdims=True), jnp.max(high, axis=0, keepdims=True)

    def weigh(u, top, total):
        o, k = u // KV, u % KV
        inverse = 1.0 / total
        out = None
        for a in range(0, PADDED, 2 * DIM):
            n = min(2 * DIM, PADDED - a)
            p = (e_ref[u, a : a + n, :] * inverse).astype(BF16)
            if n < 2 * DIM:
                p = jnp.concatenate([p, jnp.zeros((DEEP - a - n, SPAN), BF16)], axis=0)
            part = dot(turned_v[o, k, :, a : a + p.shape[0]], p)
            out = part if out is None else out + part
        o_ref[o, k] = out
        put_rows(m_ref, o, k, top * SCALE)
        put_rows(w_ref, o, k, top * SCALE + jnp.log(total))

    def ready_q(o, k):
        if o == 0:
            q_arrived(1, k)

        @pl.when(inner)
        def _():
            q_arrived(2 + o, k)

        prep_q(o, k, 3 + o)

    loads[1].wait()
    ready_q(0, 0)
    _, top = sweep(None, 0, None)
    start_where(outer, q_far[1])
    ready_q(0, 1)

    @pl.when(inner)
    def _():
        for c in q_far:
            c.wait_send()
        g_far.start()

    for u in range(2 * KV):
        total, ahead = sweep(u, u + 1 if u + 1 < 2 * KV else None, top)
        weigh(u, top, total)
        top = ahead
        if u + 2 < 2 * KV:
            ready_q((u + 2) // KV, (u + 2) % KV)
        if u == 0:

            @pl.when(outer)
            def _():
                for c in q_far:
                    c.wait_send()
                g_far.start()

    loads[2].wait()
    g_arrived(1)

    @pl.when(inner)
    def _():
        g_arrived(2)
        g_arrived(3)

    for o in range(2):

        def delta(hc, carry):
            x = chosen(gbuf, o, 3 + o, pl.ds(pl.multiple_of(hc * ROWS, ROWS), ROWS))
            k, c = hc // (PER // 2), hc % (PER // 2)
            out = o_ref[o, k, :, pl.ds(pl.multiple_of(c * ROWS, ROWS), ROWS)]
            for h in range(2):
                part = slice(h * TEXT, (h + 1) * TEXT)
                put = pl.ds(pl.multiple_of(c * ROWS + h * TEXT, TEXT), TEXT)
                raw = x[:, part]
                turned_raw = raw.T
                grad = (gate * turned_raw).astype(BF16)
                gs[o, k, put, :] = (gate * raw).astype(BF16)
                gsT[o, k, :, put] = grad
                at = pl.ds(2 * hc + h, 1)
                d_ref[o, at, :] = jnp.sum(out[:, part] * grad.astype(F32), axis=0, keepdims=True)
                gam_ref[o, at, :] = jnp.sum(out[:, part] * turned_raw, axis=0, keepdims=True)
            return carry

        lax.fori_loop(0, CHUNKS, delta, 0)
        saw = jnp.broadcast_to(seen[o], (HEADS, TEXT)) > 0.0
        stats[j, slot_of(o), 0] = jnp.where(saw, w_ref[o], NEGATIVE)
        stats[j, slot_of(o), 1] = jnp.where(saw, d_ref[o], 0.0)

    swaps = []
    for step in range(1, GROUP):
        swaps.append(
            remote(
                stats.at[j], stats.at[j], stat_send.at[step - 1], stat_recv.at[j],
                base + (j + step) % GROUP,
            )
        )
    for c in swaps:
        c.start()
    for step in range(1, GROUP):
        other = (j + step) % GROUP
        remote(stats.at[j], stats.at[other], stat_send.at[0], stat_recv.at[other], near).wait_recv()

    gate_sum = jnp.zeros((HEADS, TEXT), F32)
    for o in range(2):
        mine = [img_ref[2 * base + i] - base == docs[o] for i in range(2 * GROUP)]
        lses = [
            jnp.where(mine[i], stats[i // 2, i % 2, 0], 2.0 * NEGATIVE) for i in range(2 * GROUP)
        ]
        top = functools.reduce(jnp.maximum, lses)
        terms = [jnp.exp(x - top) for x in lses]
        total = functools.reduce(jnp.add, terms)
        weighted = [
            t * jnp.where(mine[i], stats[i // 2, i % 2, 1], 0.0) for i, t in enumerate(terms)
        ]
        saw = jnp.broadcast_to(seen[o], (HEADS, TEXT)) > 0.0
        own = jnp.where(saw, w_ref[o], NEGATIVE)
        d_ref[o] = functools.reduce(jnp.add, weighted) / total
        f_ref[o] = jnp.where(saw, jnp.exp(m_ref[o] - (top + jnp.log(total))), 0.0)
        w_ref[o] = jnp.where(saw, jnp.exp(own - top) / total, 0.0)
        gate_sum = gate_sum + w_ref[o] * gam_ref[o]

    def share(pair, own_b, near_b, far_b, k, lanes):
        def total(r):
            a = jnp.where(rels[0] == r, pair[0], 0.0)
            return a + jnp.where(rels[1] == r, pair[1], 0.0)

        own_b[k, :, lanes] = total(0)
        near_b[k, :, lanes] = total(1)
        far_b[0, k, :, lanes] = total(2).astype(BF16)
        far_b[1, k, :, lanes] = total(3).astype(BF16)

    def returns(which, k, near_b, far_b, rnear_b, rfar_b):
        one = remote(
            near_b.at[k], rnear_b.at[k], ret_send.at[which, k, 0], ret_recv.at[which, k, 0], near
        )
        two = [
            remote(
                far_b.at[r, k], rfar_b.at[k], ret_send.at[which, k, 1 + r],
                ret_recv.at[which, k, 1], base + jnp.where(j == 1, 2 + r, 1 - r),
            )
            for r in range(2)
        ]
        return one, two

    def start_returns(*args):
        one, two = returns(*args)
        one.start()

        @pl.when(inner)
        def _():
            for c in two:
                c.start()

    def finish_sends(*args):
        one, two = returns(*args)
        one.wait_send()

        @pl.when(inner)
        def _():
            for c in two:
                c.wait_send()

    def wait_returns(*args):
        one, two = returns(*args)
        one.wait_recv()
        two[0].wait_recv()

    o_args = (near_o, far_o, rnear_o, rfar_o)
    q_args = (near_q, far_q, rnear_q, rfar_q)

    def give_out(k, carry):
        def body(c, carry):
            hc = k * (PER // 2) + c
            pair = []
            for o in range(2):
                w = [w_ref[o, pl.ds(2 * hc + h, 1), :] for h in range(2)]
                x = o_ref[o, k, :, pl.ds(pl.multiple_of(c * ROWS, ROWS), ROWS)]
                x = x * jnp.concatenate(w, axis=1)
                pair.append(jnp.concatenate([x[:, :TEXT].T, x[:, TEXT:].T], axis=1))
            share(pair, own_o, near_o, far_o, k, pl.ds(pl.multiple_of(c * ROWS, ROWS), ROWS))
            return carry

        lax.fori_loop(0, PER // 2, body, 0)
        start_returns(0, k, *o_args)
        return carry

    lax.fori_loop(0, KV, give_out, 0)

    def backward(k, sums):
        kgain_sum, qgain_sum = sums

        def per_slot(o, carry):
            factor = get_rows(f_ref, o, k)
            delta = get_rows(d_ref, o, k)
            for a in range(0, PADDED, 2 * DIM):
                n = min(2 * DIM, PADDED - a)
                dp = dot(vpad[o, k, a : a + n, :], gsT[o, k])
                p = e_ref[2 * o + k, a : a + n, :] * factor
                ds = (p * (dp - delta)).astype(BF16)
                value = dot(p.astype(BF16), gs[o, k])
                e_ref[2 * o + k, a : a + n, :DIM] = dot(ds, qh[o, k])
                if n < 2 * DIM:
                    ds = jnp.concatenate([ds, jnp.zeros((DEEP - a - n, SPAN), BF16)], axis=0)
                part = dot(turned_k[o, k, :, a : a + ds.shape[0]], ds)
                if a == 0:
                    x_acc[...] = part
                else:
                    x_acc[...] += part
                whole = min(n, MAIN - a)
                wide_v[rows_of(o, k, a, whole), :] = value[:whole]
                if whole < n:
                    wide_v[pl.ds(4 * MAIN + 2 * k + slot_of(o), 1), :] = value[whole : whole + 1]
            for c in range(PER // 2):
                dq_ref[o, c] = jnp.concatenate(
                    [x_acc[:, c * ROWS + h * TEXT : c * ROWS + (h + 1) * TEXT].T for h in range(2)], axis=1
                )
            return carry

        lax.fori_loop(0, 2, per_slot, 0)

        def body(c, qgain_sum):
            pair = [dq_ref[0, c], dq_ref[1, c]]
            share(pair, own_q, near_q, far_q, k, pl.ds(pl.multiple_of(c * ROWS, ROWS), ROWS))
            full = pl.ds(pl.multiple_of(k * PER * DIM + c * ROWS, ROWS), ROWS)
            for o in range(2):
                x = chosen(qbuf, o, 3 + o, full)
                for h in range(2):
                    part = slice(h * DIM, (h + 1) * DIM)
                    unit, _ = unit_of(x[:, part])
                    qgain_sum = qgain_sum + fold(pair[o][:, part] * unit, jnp.sum)
            return qgain_sum

        qgain_sum = lax.fori_loop(0, PER // 2, body, qgain_sum)
        start_returns(1, k, *q_args)

        def norm_back(o, kgain_sum):
            def key_step(x, up, kgain_sum):
                up = up * SCALE
                unit, inverse = unit_of(x)
                scaled = up * kgain_ref[...]
                back = inverse * (scaled - unit * jnp.mean(scaled * unit, axis=1, keepdims=True))
                return back, kgain_sum + fold(up * unit, jnp.sum)

            for a in range(0, MAIN, STEP):
                at = rows_of(o, k, a, STEP)
                back, kgain_sum = key_step(wide_k[at, :], e_ref[2 * o + k, a : a + STEP, :DIM], kgain_sum)
                wide_k[at, :] = back
            back, kgain_sum = key_step(
                tail_of(wide_k, o, k), e_ref[2 * o + k, MAIN:PADDED, :DIM], kgain_sum
            )
            wide_k[pl.ds(4 * MAIN + 2 * k + slot_of(o), 1), :] = back[:1]
            return kgain_sum

        return lax.fori_loop(0, 2, norm_back, kgain_sum), qgain_sum

    zero = jnp.zeros((8, DIM), F32)
    kgain_sum, qgain_sum = lax.fori_loop(0, KV, backward, (zero, zero))

    row = lax.broadcasted_iota(jnp.int32, (8, DIM), 0)
    gate_total = jnp.sum(jnp.sum(gate_sum, axis=0, keepdims=True), axis=1, keepdims=True)
    part = jnp.where(
        row == 0,
        jnp.sum(qgain_sum, axis=0, keepdims=True) * SCALE,
        jnp.where(
            row == 1,
            jnp.sum(kgain_sum, axis=0, keepdims=True),
            (1.0 - gate * gate) * gate_total,
        ),
    )

    def stage_copies(n):
        axis, stride, count, mine, low = place(stages[n])
        buf = sum_bufs[n]
        out, come = [], []
        for step in range(1, count):
            other = (mine + step) % count
            for at, to, found in ((mine, out, step), (other, come, 0)):
                to.append(
                    pltpu.make_async_remote_copy(
                        src_ref=buf.at[at], dst_ref=buf.at[at], send_sem=sum_send.at[n, found],
                        recv_sem=sum_recv.at[n, at], device_id={axis: low + stride * other},
                        device_id_type=MESH,
                    )
                )
        return out, come

    def stage_start(n, value):
        sum_bufs[n][place(stages[n])[3]] = value
        for c in stage_copies(n)[0]:
            c.start()

    def stage_end(n):
        for c in stage_copies(n)[1]:
            c.wait_recv()
        value = sum_bufs[n][0]
        for i in range(1, stages[n][2]):
            value = value + sum_bufs[n][i]
        return value

    stage_start(0, part)

    outs = [
        pltpu.make_async_copy(kraw, dk_hbm, out_sem.at[0]),
        pltpu.make_async_copy(vraw, dv_hbm, out_sem.at[1]),
    ]
    narrow(wide_k, kraw)
    outs[0].start()
    narrow(wide_v, vraw)
    outs[1].start()
    part = stage_end(0)
    if len(stages) > 1:
        stage_start(1, part)

    for k in range(KV):
        wait_returns(0, k, *o_args)

    def attend(k, carry):
        for c in range(PER):
            lanes = slice(c * DIM, (c + 1) * DIM)
            full = pl.ds(pl.multiple_of(k * PER * DIM + c * DIM, DIM), DIM)
            merged = own_o[k, :, lanes] + rnear_o[k, :, lanes] + rfar_o[k, :, lanes].astype(F32)
            gbuf[0, :, full] = (gate * merged).astype(BF16)
        return carry

    lax.fori_loop(0, KV, attend, 0)
    out_att = pltpu.make_async_copy(gbuf.at[0], att_hbm.at[0], out_sem.at[4])
    out_att.start()
    if len(stages) > 1:
        part = stage_end(1)
    if len(stages) > 2:
        stage_start(2, part)

    for k in range(KV):
        wait_returns(1, k, *q_args)

    def finish(k, carry):
        for c in range(PER):
            lanes = slice(c * DIM, (c + 1) * DIM)
            full = pl.ds(pl.multiple_of(k * PER * DIM + c * DIM, DIM), DIM)
            hat = own_q[k, :, lanes] + rnear_q[k, :, lanes] + rfar_q[k, :, lanes].astype(F32)
            hat = hat * SCALE
            unit, inverse = unit_of(qbuf[0, :, full].astype(F32))
            scaled = hat * qgain_ref[...]
            back = inverse * (scaled - unit * jnp.mean(scaled * unit, axis=1, keepdims=True))
            qbuf[0, :, full] = back.astype(BF16)
        return carry

    lax.fori_loop(0, KV, finish, 0)
    out_dq = pltpu.make_async_copy(qbuf.at[0], dq_hbm.at[0], out_sem.at[5])
    out_dq.start()

    if len(stages) > 2:
        part = stage_end(2)
    qg_out[...] = part[0:1]
    kg_out[...] = part[1:2]
    gate_out[...] = part[2:3, 0:1]
    for n in range(len(stages)):
        for c in stage_copies(n)[0]:
            c.wait_send()
    for c in (*q_near, g_near, g_far):
        c.wait_send()
    for c in swaps:
        c.wait_send()
    for k in range(KV):
        finish_sends(0, k, *o_args)
        finish_sends(1, k, *q_args)
    for c in outs:
        c.wait()
    out_att.wait()
    out_dq.wait()


def run_main(stages, img, gate, qgain, kgain, text_mask, q, g, kk, vv):
    vm = pltpu.VMEM
    dma = pltpu.SemaphoreType.DMA
    half = (KV, TEXT, PER * DIM)
    slots = text_mask.shape[0]
    scratch = [
        vm((slots, 8, TEXT), jnp.int32),
        vm((4, TEXT, HEADS * DIM), BF16),
        vm((4, TEXT, HEADS * DIM), BF16),
        vm((COLS, 4, DIM), BF16),
        vm((COLS, 4, DIM), BF16),
        vm((4 * PADDED, DIM), F32),
        vm((4 * PADDED, DIM), F32),
        vm((2, KV, PADDED, DIM), BF16),
        vm((2, KV, PADDED, DIM), BF16),
        vm((2, KV, DIM, DEEP), BF16),
        vm((2, KV, DIM, DEEP), BF16),
        vm((2, KV, SPAN, DIM), BF16),
        vm((2, KV, DIM, SPAN), BF16),
        vm((2, KV, SPAN, DIM), BF16),
        vm((2, KV, DIM, SPAN), BF16),
        vm((2 * KV, PADDED, SPAN), F32),
        vm((2, KV, DIM, SPAN), F32),
        vm((2, PER // 2, TEXT, ROWS), F32),
        vm((DIM, SPAN), F32),
        vm((2, HEADS, TEXT), F32),
        vm((2, HEADS, TEXT), F32),
        vm((2, HEADS, TEXT), F32),
        vm((2, HEADS, TEXT), F32),
        vm((2, HEADS, TEXT), F32),
        vm((GROUP, 2, 2, HEADS, TEXT), F32),
        vm(half, F32),
        vm(half, F32),
        vm((2,) + half, BF16),
        vm(half, F32),
        vm(half, F32),
        vm((2,) + half, BF16),
        vm(half, F32),
        vm(half, BF16),
        vm(half, F32),
        vm(half, BF16),
        dma((7,)),
        dma((6,)),
        dma((3, 4)),
        dma((3,)),
        dma((4,)),
        dma((2, KV, 3)),
        dma((2, KV, 2)),
        dma((6,)),
        dma((len(stages), max(s[2] for s in stages))),
        dma((len(stages), max(s[2] for s in stages))),
    ] + [vm((s[2], 8, DIM), F32) for s in stages]
    hbm = pl.BlockSpec(memory_space=pl.ANY)
    vmem = pl.BlockSpec(memory_space=pltpu.VMEM)
    return pl.pallas_call(
        functools.partial(main_kernel, stages),
        out_shape=(
            jax.ShapeDtypeStruct(q.shape, BF16),
            jax.ShapeDtypeStruct(q.shape, BF16),
            jax.ShapeDtypeStruct(kk.shape, BF16),
            jax.ShapeDtypeStruct(vv.shape, BF16),
            jax.ShapeDtypeStruct((1, DIM), F32),
            jax.ShapeDtypeStruct((1, DIM), F32),
            jax.ShapeDtypeStruct((1, 1), F32),
        ),
        in_specs=[pl.BlockSpec(memory_space=pltpu.SMEM), vmem, vmem, vmem] + [hbm] * 5,
        out_specs=(hbm, hbm, hbm, hbm, vmem, vmem, vmem),
        scratch_shapes=scratch,
        compiler_params=pltpu.CompilerParams(
            collective_id=0, has_side_effects=True, vmem_limit_bytes=64 * 1024 * 1024
        ),
    )(img, gate, qgain, kgain, text_mask, q, g, kk, vv)


def stages_of(sizes):
    low = min(8, sizes["dp"])
    out = [("dp", 1, low)]
    if sizes["heads"] > 1:
        out.append(("heads", 1, sizes["heads"]))
    if sizes["dp"] > low:
        out.append(("dp", low, sizes["dp"] // low))
    return out


PIECES = 4


def copy_kernel(count, *refs):
    stage = refs[2 * count : 3 * count]
    come, leave = refs[3 * count :]
    pairs = []
    for i in range(count):
        rows = refs[i].shape[0]
        size = -(-rows // PIECES)
        for n, a in enumerate(range(0, rows, size)):
            at = pl.ds(a, min(size, rows - a))
            pairs.append(
                (
                    pltpu.make_async_copy(refs[i].at[at], stage[i].at[at], come.at[i, n]),
                    pltpu.make_async_copy(stage[i].at[at], refs[count + i].at[at], leave.at[i, n]),
                )
            )
    for first, _ in pairs:
        first.start()
    for first, second in pairs:
        first.wait()
        second.start()
    for _, second in pairs:
        second.wait()


def settled(*arrays):
    hbm = pl.BlockSpec(memory_space=pl.ANY)
    count = len(arrays)
    return pl.pallas_call(
        functools.partial(copy_kernel, count),
        out_shape=tuple(jax.ShapeDtypeStruct(a.shape, a.dtype) for a in arrays),
        in_specs=[hbm] * count,
        out_specs=(hbm,) * count,
        scratch_shapes=[pltpu.VMEM(a.shape, a.dtype) for a in arrays]
        + [pltpu.SemaphoreType.DMA((count, PIECES))] * 2,
        compiler_params=pltpu.CompilerParams(vmem_limit_bytes=64 * 1024 * 1024),
    )(*arrays)


def interleaved(x):
    x = x.transpose(1, 0, 2).reshape(COLS, 2, KV, DIM)
    return x.transpose(0, 2, 1, 3).reshape(COLS, 2 * KV, DIM)


def separated(x):
    return x.reshape(COLS, KV, 2, DIM).transpose(2, 0, 1, 3).reshape(2, COLS, KV * DIM)


def solution(mesh):
    sizes = dict(mesh.shape)

    def per_device(q, qgain, kk, vv, kgain, gate, img, text_mask, g):
        found = run_main(
            stages_of(sizes), img, gate.reshape(1, 1), qgain.reshape(1, DIM),
            kgain.reshape(1, DIM), text_mask.transpose(2, 0, 1), q, g, interleaved(kk),
            interleaved(vv),
        )
        att, dq, dk, dv, qg, kg, gt = settled(*found)
        return (
            att, dq, separated(dk), separated(dv), qg.reshape(DIM), kg.reshape(DIM), gt.reshape(1)
        )

    split = P("dp", None, "heads")
    return jax.shard_map(
        per_device,
        mesh=mesh,
        in_specs=(split, P(), split, split, P(), P(), P(), P(), split),
        out_specs=(split, split, split, split, P(), P(), P()),
        check_vma=False,
    )
```

```python
import functools

import jax
import jax.numpy as jnp
from jax import lax
from jax.experimental import pallas as pl
from jax.experimental.pallas import tpu as pltpu
from jax.sharding import PartitionSpec as P

EPSILON = 1e-05
NEGATIVE = -1e30
LOG2E = 1.4426950408889634
MESH = pl.DeviceIdType.MESH
F32 = jnp.float32
BF16 = jnp.bfloat16

GROUP = 4
DIM = 128
TEXT = 128
HEADS = 16
KV = 2
PER = HEADS // KV
CHUNKS = HEADS // 2
ROWS = 2 * TEXT
SPAN = PER * TEXT
COLS = 1601
MAIN = 1600
PADDED = 1616
DEEP = 1664
SCALE = DIM ** (-0.5)


def dot(a, b):
    return jnp.dot(a, b, preferred_element_type=F32)


def crossed(a, b):
    return lax.dot_general(a, b, (((1,), (1,)), ((), ())), preferred_element_type=F32)


def fold(x, op):
    return op(x.reshape(x.shape[0] // 8, 8, x.shape[1]), axis=0)


def place(stage):
    axis, stride, count = stage
    me = lax.axis_index(axis)
    mine = (me // stride) % count
    return axis, stride, count, mine, me - mine * stride


def main_kernel(
    stages,
    img_ref,
    gate_ref,
    qgain_ref,
    kgain_ref,
    tm_hbm,
    q_hbm,
    g_hbm,
    k_hbm,
    v_hbm,
    att_hbm,
    dq_hbm,
    dk_hbm,
    dv_hbm,
    qg_out,
    kg_out,
    gate_out,
    tm_ref,
    qbuf,
    gbuf,
    kraw,
    vraw,
    wide_k,
    wide_v,
    khat,
    vpad,
    turned_k,
    turned_v,
    qh,
    qhT,
    gs,
    gsT,
    e_ref,
    o_ref,
    dq_ref,
    x_acc,
    m_ref,
    f_ref,
    d_ref,
    w_ref,
    gam_ref,
    lw_ref,
    wt_ref,
    stats,
    own_o,
    near_o,
    far_o,
    own_q,
    near_q,
    far_q,
    rnear_o,
    rfar_o,
    rnear_q,
    rfar_q,
    load_sem,
    send_sem,
    recv_sem,
    stat_send,
    stat_recv,
    ret_send,
    ret_recv,
    out_sem,
    sum_send,
    sum_recv,
    *sum_bufs,
):
    me = lax.axis_index("dp")
    group = me // GROUP
    j = me % GROUP
    base = group * GROUP
    base8 = pl.multiple_of(me // 8 * 8, 8)
    inner = (j == 1) | (j == 2)
    outer = jnp.logical_not(inner)
    near = base + j + 1 - 2 * (j % 2)
    far = base + jnp.where(j < 2, 2, 1)
    far_slot = jnp.where(inner, 2, 3)
    side = jnp.where(j < 2, 0, 1)

    def slot_of(o):
        return o + side - 2 * o * side

    loads = [pltpu.make_async_copy(tm_hbm.at[:, pl.ds(base8, 8), :], tm_ref, load_sem.at[0])]
    loads.append(pltpu.make_async_copy(q_hbm.at[0], qbuf.at[0], load_sem.at[1]))
    loads.append(pltpu.make_async_copy(g_hbm.at[0], gbuf.at[0], load_sem.at[2]))
    loads.append(pltpu.make_async_copy(k_hbm, kraw, load_sem.at[3]))
    loads.append(pltpu.make_async_copy(v_hbm, vraw, load_sem.at[4]))
    for c in loads:
        c.start()

    barrier = pltpu.get_barrier_semaphore()
    for step in range(1, GROUP):
        pl.semaphore_signal(
            barrier, inc=1, device_id={"dp": base + (j + step) % GROUP}, device_id_type=MESH
        )
    partners = GROUP - 1
    for stage in stages:
        axis, stride, count, mine, low = place(stage)
        for step in range(1, count):
            other = low + stride * ((mine + step) % count)
            pl.semaphore_signal(barrier, inc=1, device_id={axis: other}, device_id_type=MESH)
            partners += 1
    pl.semaphore_wait(barrier, partners)

    def remote(src, dst, ss, rs, dev):
        return pltpu.make_async_remote_copy(
            src_ref=src, dst_ref=dst, send_sem=ss, recv_sem=rs,
            device_id={"dp": dev}, device_id_type=MESH,
        )

    def half_of(ref, k):
        return ref.at[:, pl.ds(k * PER * DIM, PER * DIM)]

    def q_send(slot, k, ss, dev):
        return remote(
            half_of(q_hbm.at[0], k), half_of(qbuf.at[slot], k), ss, recv_sem.at[k, slot], dev
        )

    def g_send(slot, ss, dev):
        return remote(g_hbm.at[0], gbuf.at[slot], ss, recv_sem.at[2, slot], dev)

    q_near = [q_send(1, k, send_sem.at[k], near) for k in range(KV)]
    q_far = [q_send(far_slot, k, send_sem.at[2 + k], far) for k in range(KV)]
    g_near = g_send(1, send_sem.at[4], near)
    g_far = g_send(far_slot, send_sem.at[5], far)

    def start_where(condition, *copies):
        @pl.when(condition)
        def _():
            for c in copies:
                c.start()

    q_near[0].start()
    start_where(inner, q_far[0])

    def q_arrived(slot, k):
        q_send(slot, k, send_sem.at[0], near).wait_recv()

    def g_arrived(slot):
        g_send(slot, send_sem.at[0], near).wait_recv()

    docs, rels, ranks = [], [], []
    for o in range(2):
        local = 2 * j + slot_of(o)
        doc = img_ref[2 * base + local]
        rank = jnp.int32(0)
        for i in range(2 * GROUP):
            same = (img_ref[2 * base + i] == doc) & (i < local)
            rank = rank + jnp.where(same, 1, 0)
        doc = doc - base
        rel = jnp.where(
            doc == j, 0, jnp.where(doc == near - base, 1, jnp.where(doc == GROUP - 1 - j, 2, 3))
        )
        docs.append(doc)
        rels.append(rel)
        ranks.append(rank)
    gate = jnp.tanh(jnp.broadcast_to(gate_ref[...], (1, DIM)))

    @pl.when(outer)
    def _():
        for r in (2, 3):
            qbuf[r] = jnp.zeros((TEXT, HEADS * DIM), BF16)
            gbuf[r] = jnp.zeros((TEXT, HEADS * DIM), BF16)


    loads[0].wait()
    seen = []
    rank_at = lax.broadcasted_iota(jnp.int32, tm_ref.shape, 0)
    doc_at = lax.broadcasted_iota(jnp.int32, tm_ref.shape, 1)
    for o in range(2):
        hit = (rank_at == ranks[o]) & (doc_at == docs[o] + (base - base8))
        row = jnp.sum(jnp.where(hit, tm_ref[...], 0).astype(F32), axis=0)
        seen.append(jnp.sum(row, axis=0, keepdims=True))

    tail_row = lax.broadcasted_iota(jnp.int32, (PADDED - MAIN, DIM), 0) == 0

    def unit_of(x):
        inverse = lax.rsqrt(jnp.mean(x * x, axis=1, keepdims=True) + EPSILON)
        return x * inverse, inverse

    def rows_of(o, k, a, n):
        return pl.ds(4 * a + 2 * k + slot_of(o), n, stride=4)

    def tail_of(ref, o, k):
        row = ref[pl.ds(4 * MAIN + 2 * k + slot_of(o), 1), :]
        return jnp.where(tail_row, jnp.broadcast_to(row, (PADDED - MAIN, DIM)), 0.0)

    def widen(raw, wide):
        rows = raw.reshape(4 * COLS, DIM)

        def body(i, carry):
            at = pl.ds(pl.multiple_of(i * 320, 320), 320)
            wide[at, :] = rows[at, :].astype(F32)
            return carry

        lax.fori_loop(0, 4 * MAIN // 320, body, 0)
        wide[4 * MAIN : 4 * COLS, :] = rows[4 * MAIN : 4 * COLS, :].astype(F32)

    def narrow(wide, raw):
        rows = raw.reshape(4 * COLS, DIM)

        def body(i, carry):
            at = pl.ds(pl.multiple_of(i * 320, 320), 320)
            rows[at, :] = wide[at, :].astype(BF16)
            return carry

        lax.fori_loop(0, 4 * MAIN // 320, body, 0)
        rows[4 * MAIN : 4 * COLS, :] = wide[4 * MAIN : 4 * COLS, :].astype(BF16)

    loads[3].wait()
    widen(kraw, wide_k)

    q_near[1].start()
    start_where(inner, q_far[1])
    loads[4].wait()
    widen(vraw, wide_v)

    def prep_kv(u, carry):
        o, k = u // KV, u % KV
        for a in range(0, DEEP, DIM):
            if a + DIM < MAIN:
                x = wide_k[rows_of(o, k, a, DIM), :]
                v = wide_v[rows_of(o, k, a, DIM), :]
                n = DIM
            else:
                n = PADDED - a
                fill = jnp.zeros((DIM - n, DIM), F32)
                x = [wide_k[rows_of(o, k, a, MAIN - a), :], tail_of(wide_k, o, k), fill]
                v = [wide_v[rows_of(o, k, a, MAIN - a), :], tail_of(wide_v, o, k), fill]
                x, v = jnp.concatenate(x, axis=0), jnp.concatenate(v, axis=0)
            unit, _ = unit_of(x)
            hat = unit * kgain_ref[...]
            khat[o, k, a : a + n, :] = hat.astype(BF16)[:n]
            vpad[o, k, a : a + n, :] = v.astype(BF16)[:n]
            turned_k[o, k, :, a : a + DIM] = hat.T.astype(BF16)
            turned_v[o, k, :, a : a + DIM] = v.T.astype(BF16)
        return carry

    lax.fori_loop(0, 2 * KV, prep_kv, 0)

    start_where(outer, q_far[0])
    g_near.start()

    def chosen(buf, o, count, lanes):
        x = buf[0, :, lanes].astype(F32)
        for r in range(1, count):
            x = jnp.where(rels[o] == r, buf[r, :, lanes].astype(F32), x)
        return x

    def prep_q(o, k, count):
        def body(c, carry):
            hc = k * (PER // 2) + c
            x = chosen(qbuf, o, count, pl.ds(pl.multiple_of(hc * ROWS, ROWS), ROWS))
            for h in range(2):
                unit, _ = unit_of(x[:, h * DIM : (h + 1) * DIM])
                hat = unit * qgain_ref[...]
                at = pl.ds(pl.multiple_of(c * ROWS + h * TEXT, TEXT), TEXT)
                qh[o, k, at, :] = hat.astype(BF16)
                qhT[o, k, :, at] = hat.T.astype(BF16)
            return carry

        lax.fori_loop(0, PER // 2, body, 0, unroll=2)

    def put_rows(ref, o, k, row):
        for h in range(PER):
            ref[o, k * PER + h : k * PER + h + 1, :] = row[:, h * TEXT : (h + 1) * TEXT]

    def get_rows(ref, o, k):
        rows = ref[o, pl.ds(pl.multiple_of(k * PER, PER), PER), :]
        return jnp.concatenate([rows[h : h + 1] for h in range(PER)], axis=1)

    tail_mask = lax.broadcasted_iota(jnp.int32, (PADDED - MAIN, SPAN), 0) == 0
    STEP = 400

    def score_step(u, at, n, top):
        o, k = u // KV, u % KV
        s = dot(khat[o, k, at, :], qhT[o, k])
        if n < STEP:
            s = jnp.where(tail_mask, s, -jnp.inf)
        e_ref[u, at, :] = s
        return jnp.maximum(top, fold(s, jnp.max))

    def exp_step(u, at, top, total):
        e = jnp.exp2((e_ref[u, at, :] - top) * (SCALE * LOG2E))
        e_ref[u, at, :] = e
        return total + fold(e, jnp.sum)

    lowest = jnp.full((8, SPAN), -jnp.inf, F32)
    nothing = jnp.zeros((8, SPAN), F32)

    def sweep(now, ahead, top):
        def body(i, carry):
            total, high = carry
            at = pl.ds(pl.multiple_of(i * STEP, STEP), STEP)
            if ahead is not None:
                high = score_step(ahead, at, STEP, high)
            if now is not None:
                total = exp_step(now, at, top, total)
            return total, high

        total, high = lax.fori_loop(0, MAIN // STEP, body, (nothing, lowest))
        at = slice(MAIN, PADDED)
        if ahead is not None:
            high = score_step(ahead, at, PADDED - MAIN, high)
        if now is not None:
            total = exp_step(now, at, top, total)
        return jnp.sum(total, axis=0, keepdims=True), jnp.max(high, axis=0, keepdims=True)

    def weigh(u, top, total):
        o, k = u // KV, u % KV
        inverse = 1.0 / total
        out = None
        for a in range(0, PADDED, 2 * DIM):
            n = min(2 * DIM, PADDED - a)
            p = (e_ref[u, a : a + n, :] * inverse).astype(BF16)
            if n < 2 * DIM:
                p = jnp.concatenate([p, jnp.zeros((DEEP - a - n, SPAN), BF16)], axis=0)
            part = dot(turned_v[o, k, :, a : a + p.shape[0]], p)
            out = part if out is None else out + part
        o_ref[o, k] = out
        put_rows(m_ref, o, k, top * SCALE)
        put_rows(w_ref, o, k, top * SCALE + jnp.log(total))

    def ready_q(o, k):
        if o == 0:
            q_arrived(1, k)

        @pl.when(inner)
        def _():
            q_arrived(2 + o, k)

        prep_q(o, k, 3 + o)

    loads[1].wait()
    ready_q(0, 0)
    _, top = sweep(None, 0, None)
    start_where(outer, q_far[1])
    ready_q(0, 1)

    g_far.start()

    for u in range(2 * KV):
        total, ahead = sweep(u, u + 1 if u + 1 < 2 * KV else None, top)
        weigh(u, top, total)
        top = ahead
        if u + 2 < 2 * KV:
            ready_q((u + 2) // KV, (u + 2) % KV)
    loads[2].wait()
    g_arrived(1)

    @pl.when(inner)
    def _():
        g_arrived(2)
        g_arrived(3)

    for o in range(2):

        def delta(hc, carry):
            x = chosen(gbuf, o, 3 + o, pl.ds(pl.multiple_of(hc * ROWS, ROWS), ROWS))
            k, c = hc // (PER // 2), hc % (PER // 2)
            out = o_ref[o, k, :, pl.ds(pl.multiple_of(c * ROWS, ROWS), ROWS)]
            for h in range(2):
                part = slice(h * TEXT, (h + 1) * TEXT)
                put = pl.ds(pl.multiple_of(c * ROWS + h * TEXT, TEXT), TEXT)
                raw = x[:, part]
                turned_raw = raw.T
                grad = (gate * turned_raw).astype(BF16)
                gs[o, k, put, :] = (gate * raw).astype(BF16)
                gsT[o, k, :, put] = grad
                at = pl.ds(2 * hc + h, 1)
                d_ref[o, at, :] = jnp.sum(out[:, part] * grad.astype(F32), axis=0, keepdims=True)
                gam_ref[o, at, :] = jnp.sum(out[:, part] * turned_raw, axis=0, keepdims=True)
            return carry

        lax.fori_loop(0, CHUNKS, delta, 0, unroll=2)
        saw = jnp.broadcast_to(seen[o], (HEADS, TEXT)) > 0.0
        stats[j, slot_of(o), 0] = jnp.where(saw, w_ref[o], NEGATIVE)
        stats[j, slot_of(o), 1] = jnp.where(saw, d_ref[o], 0.0)

    swaps = []
    for step in range(1, GROUP):
        swaps.append(
            remote(
                stats.at[j], stats.at[j], stat_send.at[step - 1], stat_recv.at[j],
                base + (j + step) % GROUP,
            )
        )
    for c in swaps:
        c.start()

    saws = [jnp.broadcast_to(seen[o], (HEADS, TEXT)) > 0.0 for o in range(2)]
    mine_lse = [jnp.where(saws[o], w_ref[o], NEGATIVE) for o in range(2)]
    peak = jnp.maximum(mine_lse[0], mine_lse[1])
    shares = [jnp.exp(x - peak) for x in mine_lse]
    for o in range(2):
        local = jnp.where(rels[0] == rels[1], shares[o] / (shares[0] + shares[1]), 1.0)
        lw_ref[o] = jnp.where(saws[o], local, 0.0)

    def share(pair, own_b, near_b, far_b, k, lanes):
        def total(r):
            a = jnp.where(rels[0] == r, pair[0], 0.0)
            return a + jnp.where(rels[1] == r, pair[1], 0.0)

        own_b[k, :, lanes] = total(0)
        near_b[k, :, lanes] = total(1)
        far_b[0, k, :, lanes] = total(2).astype(BF16)
        far_b[1, k, :, lanes] = total(3).astype(BF16)

    def returns(which, k, near_b, far_b, rnear_b, rfar_b):
        one = remote(
            near_b.at[k], rnear_b.at[k], ret_send.at[which, k, 0], ret_recv.at[which, k, 0], near
        )
        two = [
            remote(
                far_b.at[r, k], rfar_b.at[k], ret_send.at[which, k, 1 + r],
                ret_recv.at[which, k, 1], base + jnp.where(j == 1, 2 + r, 1 - r),
            )
            for r in range(2)
        ]
        return one, two

    def start_returns(*args):
        one, two = returns(*args)
        one.start()

        @pl.when(inner)
        def _():
            for c in two:
                c.start()

    def finish_sends(*args):
        one, two = returns(*args)
        one.wait_send()

        @pl.when(inner)
        def _():
            for c in two:
                c.wait_send()

    def wait_returns(*args):
        one, two = returns(*args)
        one.wait_recv()
        two[0].wait_recv()

    o_args = (near_o, far_o, rnear_o, rfar_o)
    q_args = (near_q, far_q, rnear_q, rfar_q)

    def give_out(k, carry):
        def body(c, carry):
            hc = k * (PER // 2) + c
            pair = []
            for o in range(2):
                w = [lw_ref[o, pl.ds(2 * hc + h, 1), :] for h in range(2)]
                x = o_ref[o, k, :, pl.ds(pl.multiple_of(c * ROWS, ROWS), ROWS)]
                x = x * jnp.concatenate(w, axis=1)
                pair.append(jnp.concatenate([x[:, :TEXT].T, x[:, TEXT:].T], axis=1))
            share(pair, own_o, near_o, far_o, k, pl.ds(pl.multiple_of(c * ROWS, ROWS), ROWS))
            return carry

        lax.fori_loop(0, PER // 2, body, 0, unroll=2)
        start_returns(0, k, *o_args)
        return carry

    lax.fori_loop(0, KV, give_out, 0)

    for step in range(1, GROUP):
        other = (j + step) % GROUP
        remote(stats.at[j], stats.at[other], stat_send.at[0], stat_recv.at[other], near).wait_recv()

    def of_document(doc):
        mine = [img_ref[2 * base + i] - base == doc for i in range(2 * GROUP)]
        lses = [
            jnp.where(mine[i], stats[i // 2, i % 2, 0], 2.0 * NEGATIVE) for i in range(2 * GROUP)
        ]
        top = functools.reduce(jnp.maximum, lses)
        terms = [jnp.exp(x - top) for x in lses]
        return mine, top, terms, functools.reduce(jnp.add, terms)

    _, _, terms, total = of_document(j)
    for r, holder in enumerate((j, near - base, far - base)):
        weight = jnp.zeros((HEADS, TEXT), F32)
        for i in range(2 * GROUP):
            weight = weight + jnp.where(holder == i // 2, terms[i], 0.0)
        fill = jnp.zeros((DIM - HEADS, TEXT), F32)
        wt_ref[r] = jnp.concatenate([weight / total, fill], axis=0).T

    gate_sum = jnp.zeros((HEADS, TEXT), F32)
    for o in range(2):
        mine, top, terms, total = of_document(docs[o])
        weighted = [
            t * jnp.where(mine[i], stats[i // 2, i % 2, 1], 0.0) for i, t in enumerate(terms)
        ]
        saw = jnp.broadcast_to(seen[o], (HEADS, TEXT)) > 0.0
        own = jnp.where(saw, w_ref[o], NEGATIVE)
        d_ref[o] = functools.reduce(jnp.add, weighted) / total
        f_ref[o] = jnp.where(saw, jnp.exp(m_ref[o] - (top + jnp.log(total))), 0.0)
        w_ref[o] = jnp.where(saw, jnp.exp(own - top) / total, 0.0)
        gate_sum = gate_sum + w_ref[o] * gam_ref[o]

    def backward(k, sums):
        kgain_sum, qgain_sum = sums

        def per_slot(o, carry):
            factor = get_rows(f_ref, o, k)
            delta = get_rows(d_ref, o, k)
            for a in range(0, PADDED, 2 * DIM):
                n = min(2 * DIM, PADDED - a)
                dp = dot(vpad[o, k, a : a + n, :], gsT[o, k])
                p = e_ref[2 * o + k, a : a + n, :] * factor
                ds = (p * (dp - delta)).astype(BF16)
                value = crossed(gsT[o, k], p.astype(BF16)).T
                e_ref[2 * o + k, a : a + n, :DIM] = crossed(qhT[o, k], ds).T
                if n < 2 * DIM:
                    ds = jnp.concatenate([ds, jnp.zeros((DEEP - a - n, SPAN), BF16)], axis=0)
                part = dot(turned_k[o, k, :, a : a + ds.shape[0]], ds)
                if a == 0:
                    x_acc[...] = part
                else:
                    x_acc[...] += part
                whole = min(n, MAIN - a)
                wide_v[rows_of(o, k, a, whole), :] = value[:whole]
                if whole < n:
                    wide_v[pl.ds(4 * MAIN + 2 * k + slot_of(o), 1), :] = value[whole : whole + 1]
            for c in range(PER // 2):
                dq_ref[o, c] = jnp.concatenate(
                    [x_acc[:, c * ROWS + h * TEXT : c * ROWS + (h + 1) * TEXT].T for h in range(2)], axis=1
                )
            return carry

        lax.fori_loop(0, 2, per_slot, 0)

        def body(c, qgain_sum):
            pair = [dq_ref[0, c], dq_ref[1, c]]
            share(pair, own_q, near_q, far_q, k, pl.ds(pl.multiple_of(c * ROWS, ROWS), ROWS))
            full = pl.ds(pl.multiple_of(k * PER * DIM + c * ROWS, ROWS), ROWS)
            for o in range(2):
                x = chosen(qbuf, o, 3 + o, full)
                for h in range(2):
                    part = slice(h * DIM, (h + 1) * DIM)
                    unit, _ = unit_of(x[:, part])
                    qgain_sum = qgain_sum + fold(pair[o][:, part] * unit, jnp.sum)
            return qgain_sum

        qgain_sum = lax.fori_loop(0, PER // 2, body, qgain_sum, unroll=2)
        start_returns(1, k, *q_args)

        def norm_back(o, kgain_sum):
            def key_step(x, up, kgain_sum):
                up = up * SCALE
                unit, inverse = unit_of(x)
                scaled = up * kgain_ref[...]
                back = inverse * (scaled - unit * jnp.mean(scaled * unit, axis=1, keepdims=True))
                return back, kgain_sum + fold(up * unit, jnp.sum)

            for a in range(0, MAIN, STEP):
                at = rows_of(o, k, a, STEP)
                back, kgain_sum = key_step(wide_k[at, :], e_ref[2 * o + k, a : a + STEP, :DIM], kgain_sum)
                wide_k[at, :] = back
            back, kgain_sum = key_step(
                tail_of(wide_k, o, k), e_ref[2 * o + k, MAIN:PADDED, :DIM], kgain_sum
            )
            wide_k[pl.ds(4 * MAIN + 2 * k + slot_of(o), 1), :] = back[:1]
            return kgain_sum

        return lax.fori_loop(0, 2, norm_back, kgain_sum), qgain_sum

    zero = jnp.zeros((8, DIM), F32)
    kgain_sum, qgain_sum = lax.fori_loop(0, KV, backward, (zero, zero))

    row = lax.broadcasted_iota(jnp.int32, (8, DIM), 0)
    gate_total = jnp.sum(jnp.sum(gate_sum, axis=0, keepdims=True), axis=1, keepdims=True)
    part = jnp.where(
        row == 0,
        jnp.sum(qgain_sum, axis=0, keepdims=True) * SCALE,
        jnp.where(
            row == 1,
            jnp.sum(kgain_sum, axis=0, keepdims=True),
            (1.0 - gate * gate) * gate_total,
        ),
    )

    def stage_copies(n):
        axis, stride, count, mine, low = place(stages[n])
        buf = sum_bufs[n]
        out, come = [], []
        for step in range(1, count):
            other = (mine + step) % count
            for at, to, found in ((mine, out, step), (other, come, 0)):
                to.append(
                    pltpu.make_async_remote_copy(
                        src_ref=buf.at[at], dst_ref=buf.at[at], send_sem=sum_send.at[n, found],
                        recv_sem=sum_recv.at[n, at], device_id={axis: low + stride * other},
                        device_id_type=MESH,
                    )
                )
        return out, come

    def stage_start(n, value):
        sum_bufs[n][place(stages[n])[3]] = value
        for c in stage_copies(n)[0]:
            c.start()

    def stage_end(n):
        for c in stage_copies(n)[1]:
            c.wait_recv()
        value = sum_bufs[n][0]
        for i in range(1, stages[n][2]):
            value = value + sum_bufs[n][i]
        return value

    stage_start(0, part)

    outs = [
        pltpu.make_async_copy(kraw, dk_hbm, out_sem.at[0]),
        pltpu.make_async_copy(vraw, dv_hbm, out_sem.at[1]),
    ]
    narrow(wide_k, kraw)
    outs[0].start()
    narrow(wide_v, vraw)
    outs[1].start()
    part = stage_end(0)
    if len(stages) > 1:
        stage_start(1, part)

    for k in range(KV):
        wait_returns(0, k, *o_args)

    for h in range(HEADS):
        k, lanes = h // PER, slice(h % PER * DIM, (h % PER + 1) * DIM)
        parts = (own_o[k, :, lanes], rnear_o[k, :, lanes], rfar_o[k, :, lanes].astype(F32))
        merged = functools.reduce(
            jnp.add, [wt_ref[r, :, h : h + 1] * x for r, x in enumerate(parts)]
        )
        gbuf[0, :, h * DIM : (h + 1) * DIM] = (gate * merged).astype(BF16)
    out_att = pltpu.make_async_copy(gbuf.at[0], att_hbm.at[0], out_sem.at[4])
    out_att.start()
    if len(stages) > 1:
        part = stage_end(1)
    if len(stages) > 2:
        stage_start(2, part)

    for k in range(KV):
        wait_returns(1, k, *q_args)

    def finish(k, carry):
        for c in range(PER):
            lanes = slice(c * DIM, (c + 1) * DIM)
            full = pl.ds(pl.multiple_of(k * PER * DIM + c * DIM, DIM), DIM)
            hat = own_q[k, :, lanes] + rnear_q[k, :, lanes] + rfar_q[k, :, lanes].astype(F32)
            hat = hat * SCALE
            unit, inverse = unit_of(qbuf[0, :, full].astype(F32))
            scaled = hat * qgain_ref[...]
            back = inverse * (scaled - unit * jnp.mean(scaled * unit, axis=1, keepdims=True))
            qbuf[0, :, full] = back.astype(BF16)
        return carry

    lax.fori_loop(0, KV, finish, 0)
    out_dq = pltpu.make_async_copy(qbuf.at[0], dq_hbm.at[0], out_sem.at[5])
    out_dq.start()

    if len(stages) > 2:
        part = stage_end(2)
    qg_out[...] = part[0:1]
    kg_out[...] = part[1:2]
    gate_out[...] = part[2:3, 0:1]
    for n in range(len(stages)):
        for c in stage_copies(n)[0]:
            c.wait_send()
    for c in (*q_near, *q_far, g_near, g_far):
        c.wait_send()
    for c in swaps:
        c.wait_send()
    for k in range(KV):
        finish_sends(0, k, *o_args)
        finish_sends(1, k, *q_args)
    for c in outs:
        c.wait()
    out_att.wait()
    out_dq.wait()


def run_main(stages, img, gate, qgain, kgain, text_mask, q, g, kk, vv):
    vm = pltpu.VMEM
    dma = pltpu.SemaphoreType.DMA
    half = (KV, TEXT, PER * DIM)
    slots = text_mask.shape[0]
    scratch = [
        vm((slots, 8, TEXT), jnp.int32),
        vm((4, TEXT, HEADS * DIM), BF16),
        vm((4, TEXT, HEADS * DIM), BF16),
        vm((COLS, 4, DIM), BF16),
        vm((COLS, 4, DIM), BF16),
        vm((4 * PADDED, DIM), F32),
        vm((4 * PADDED, DIM), F32),
        vm((2, KV, PADDED, DIM), BF16),
        vm((2, KV, PADDED, DIM), BF16),
        vm((2, KV, DIM, DEEP), BF16),
        vm((2, KV, DIM, DEEP), BF16),
        vm((2, KV, SPAN, DIM), BF16),
        vm((2, KV, DIM, SPAN), BF16),
        vm((2, KV, SPAN, DIM), BF16),
        vm((2, KV, DIM, SPAN), BF16),
        vm((2 * KV, PADDED, SPAN), F32),
        vm((2, KV, DIM, SPAN), F32),
        vm((2, PER // 2, TEXT, ROWS), F32),
        vm((DIM, SPAN), F32),
        vm((2, HEADS, TEXT), F32),
        vm((2, HEADS, TEXT), F32),
        vm((2, HEADS, TEXT), F32),
        vm((2, HEADS, TEXT), F32),
        vm((2, HEADS, TEXT), F32),
        vm((2, HEADS, TEXT), F32),
        vm((3, TEXT, DIM), F32),
        vm((GROUP, 2, 2, HEADS, TEXT), F32),
        vm(half, F32),
        vm(half, F32),
        vm((2,) + half, BF16),
        vm(half, F32),
        vm(half, F32),
        vm((2,) + half, BF16),
        vm(half, F32),
        vm(half, BF16),
        vm(half, F32),
        vm(half, BF16),
        dma((7,)),
        dma((6,)),
        dma((3, 4)),
        dma((3,)),
        dma((4,)),
        dma((2, KV, 3)),
        dma((2, KV, 2)),
        dma((6,)),
        dma((len(stages), max(s[2] for s in stages))),
        dma((len(stages), max(s[2] for s in stages))),
    ] + [vm((s[2], 8, DIM), F32) for s in stages]
    hbm = pl.BlockSpec(memory_space=pl.ANY)
    vmem = pl.BlockSpec(memory_space=pltpu.VMEM)
    return pl.pallas_call(
        functools.partial(main_kernel, stages),
        out_shape=(
            jax.ShapeDtypeStruct(q.shape, BF16),
            jax.ShapeDtypeStruct(q.shape, BF16),
            jax.ShapeDtypeStruct(kk.shape, BF16),
            jax.ShapeDtypeStruct(vv.shape, BF16),
            jax.ShapeDtypeStruct((1, DIM), F32),
            jax.ShapeDtypeStruct((1, DIM), F32),
            jax.ShapeDtypeStruct((1, 1), F32),
        ),
        in_specs=[pl.BlockSpec(memory_space=pltpu.SMEM), vmem, vmem, vmem] + [hbm] * 5,
        out_specs=(hbm, hbm, hbm, hbm, vmem, vmem, vmem),
        scratch_shapes=scratch,
        compiler_params=pltpu.CompilerParams(
            collective_id=0, has_side_effects=True, vmem_limit_bytes=64 * 1024 * 1024
        ),
    )(img, gate, qgain, kgain, text_mask, q, g, kk, vv)


def stages_of(sizes):
    low = min(8, sizes["dp"])
    out = [("dp", 1, low)]
    if sizes["heads"] > 1:
        out.append(("heads", 1, sizes["heads"]))
    if sizes["dp"] > low:
        out.append(("dp", low, sizes["dp"] // low))
    return out


PIECES = 4


def copy_kernel(count, *refs):
    stage = refs[2 * count : 3 * count]
    come, leave = refs[3 * count :]
    pairs = []
    for i in range(count):
        rows = refs[i].shape[0]
        size = -(-rows // PIECES)
        for n, a in enumerate(range(0, rows, size)):
            at = pl.ds(a, min(size, rows - a))
            pairs.append(
                (
                    pltpu.make_async_copy(refs[i].at[at], stage[i].at[at], come.at[i, n]),
                    pltpu.make_async_copy(stage[i].at[at], refs[count + i].at[at], leave.at[i, n]),
                )
            )
    for first, _ in pairs:
        first.start()
    for first, second in pairs:
        first.wait()
        second.start()
    for _, second in pairs:
        second.wait()


def settled(*arrays):
    hbm = pl.BlockSpec(memory_space=pl.ANY)
    count = len(arrays)
    return pl.pallas_call(
        functools.partial(copy_kernel, count),
        out_shape=tuple(jax.ShapeDtypeStruct(a.shape, a.dtype) for a in arrays),
        in_specs=[hbm] * count,
        out_specs=(hbm,) * count,
        scratch_shapes=[pltpu.VMEM(a.shape, a.dtype) for a in arrays]
        + [pltpu.SemaphoreType.DMA((count, PIECES))] * 2,
        compiler_params=pltpu.CompilerParams(vmem_limit_bytes=64 * 1024 * 1024),
    )(*arrays)


def interleaved(x):
    x = x.transpose(1, 0, 2).reshape(COLS, 2, KV, DIM)
    return x.transpose(0, 2, 1, 3).reshape(COLS, 2 * KV, DIM)


def separated(x):
    return x.reshape(COLS, KV, 2, DIM).transpose(2, 0, 1, 3).reshape(2, COLS, KV * DIM)


def solution(mesh):
    sizes = dict(mesh.shape)

    def per_device(q, qgain, kk, vv, kgain, gate, img, text_mask, g):
        found = run_main(
            stages_of(sizes), img, gate.reshape(1, 1), qgain.reshape(1, DIM),
            kgain.reshape(1, DIM), text_mask.transpose(2, 0, 1), q, g, interleaved(kk),
            interleaved(vv),
        )
        att, dq, dk, dv, qg, kg, gt = settled(*found)
        return (
            att, dq, separated(dk), separated(dv), qg.reshape(DIM), kg.reshape(DIM), gt.reshape(1)
        )

    split = P("dp", None, "heads")
    return jax.shard_map(
        per_device,
        mesh=mesh,
        in_specs=(split, P(), split, split, P(), P(), P(), P(), split),
        out_specs=(split, split, split, split, P(), P(), P()),
        check_vma=False,
    )
```

```python
import functools

import jax
import jax.numpy as jnp
from jax import lax
from jax.experimental import pallas as pl
from jax.experimental.pallas import tpu as pltpu
from jax.sharding import PartitionSpec as P

EPSILON = 1e-05
NEGATIVE = -1e30
LOG2E = 1.4426950408889634
MESH = pl.DeviceIdType.MESH
F32 = jnp.float32
BF16 = jnp.bfloat16

GROUP = 4
DIM = 128
TEXT = 128
HEADS = 16
KV = 2
PER = HEADS // KV
CHUNKS = HEADS // 2
ROWS = 2 * TEXT
SPAN = PER * TEXT
COLS = 1601
MAIN = 1600
PADDED = 1616
DEEP = 1664
SCALE = DIM ** (-0.5)


def dot(a, b):
    return jnp.dot(a, b, preferred_element_type=F32)


def crossed(a, b):
    return lax.dot_general(a, b, (((1,), (1,)), ((), ())), preferred_element_type=F32)


def fold(x, op):
    return op(x.reshape(x.shape[0] // 8, 8, x.shape[1]), axis=0)


def place(stage):
    axis, stride, count = stage
    me = lax.axis_index(axis)
    mine = (me // stride) % count
    return axis, stride, count, mine, me - mine * stride


def main_kernel(
    stages,
    img_ref,
    gate_ref,
    qgain_ref,
    kgain_ref,
    tm_hbm,
    q_hbm,
    g_hbm,
    k_hbm,
    v_hbm,
    att_hbm,
    dq_hbm,
    dk_hbm,
    dv_hbm,
    qg_out,
    kg_out,
    gate_out,
    tm_ref,
    qbuf,
    gbuf,
    kraw,
    vraw,
    wide_k,
    wide_v,
    khat,
    vpad,
    turned_k,
    turned_v,
    qh,
    qhT,
    gs,
    gsT,
    e_ref,
    o_ref,
    dq_ref,
    x_acc,
    m_ref,
    f_ref,
    d_ref,
    w_ref,
    gam_ref,
    lw_ref,
    wt_ref,
    stats,
    own_o,
    near_o,
    far_o,
    own_q,
    near_q,
    far_q,
    rnear_o,
    rfar_o,
    rnear_q,
    rfar_q,
    load_sem,
    send_sem,
    recv_sem,
    stat_send,
    stat_recv,
    ret_send,
    ret_recv,
    out_sem,
    sum_send,
    sum_recv,
    *sum_bufs,
):
    me = lax.axis_index("dp")
    group = me // GROUP
    j = me % GROUP
    base = group * GROUP
    base8 = pl.multiple_of(me // 8 * 8, 8)
    inner = (j == 1) | (j == 2)
    outer = jnp.logical_not(inner)
    near = base + j + 1 - 2 * (j % 2)
    far = base + jnp.where(j < 2, 2, 1)
    far_slot = jnp.where(inner, 2, 3)
    side = jnp.where(j < 2, 0, 1)

    def slot_of(o):
        return o + side - 2 * o * side

    loads = [pltpu.make_async_copy(tm_hbm.at[:, pl.ds(base8, 8), :], tm_ref, load_sem.at[0])]
    loads.append(pltpu.make_async_copy(q_hbm.at[0], qbuf.at[0], load_sem.at[1]))
    loads.append(pltpu.make_async_copy(g_hbm.at[0], gbuf.at[0], load_sem.at[2]))
    loads.append(pltpu.make_async_copy(k_hbm, kraw, load_sem.at[3]))
    loads.append(pltpu.make_async_copy(v_hbm, vraw, load_sem.at[4]))
    for c in loads:
        c.start()

    barrier = pltpu.get_barrier_semaphore()
    for step in range(1, GROUP):
        pl.semaphore_signal(
            barrier, inc=1, device_id={"dp": base + (j + step) % GROUP}, device_id_type=MESH
        )
    partners = GROUP - 1
    for stage in stages:
        axis, stride, count, mine, low = place(stage)
        for step in range(1, count):
            other = low + stride * ((mine + step) % count)
            pl.semaphore_signal(barrier, inc=1, device_id={axis: other}, device_id_type=MESH)
            partners += 1
    pl.semaphore_wait(barrier, partners)

    def remote(src, dst, ss, rs, dev):
        return pltpu.make_async_remote_copy(
            src_ref=src, dst_ref=dst, send_sem=ss, recv_sem=rs,
            device_id={"dp": dev}, device_id_type=MESH,
        )

    def half_of(ref, k):
        return ref.at[:, pl.ds(k * PER * DIM, PER * DIM)]

    def q_send(slot, k, ss, dev):
        return remote(
            half_of(q_hbm.at[0], k), half_of(qbuf.at[slot], k), ss, recv_sem.at[k, slot], dev
        )

    def g_send(slot, ss, dev):
        return remote(g_hbm.at[0], gbuf.at[slot], ss, recv_sem.at[2, slot], dev)

    q_near = [q_send(1, k, send_sem.at[k], near) for k in range(KV)]
    q_far = [q_send(far_slot, k, send_sem.at[2 + k], far) for k in range(KV)]
    g_near = g_send(1, send_sem.at[4], near)
    g_far = g_send(far_slot, send_sem.at[5], far)

    def start_where(condition, *copies):
        @pl.when(condition)
        def _():
            for c in copies:
                c.start()

    q_near[0].start()
    start_where(inner, q_far[0])

    def q_arrived(slot, k):
        q_send(slot, k, send_sem.at[0], near).wait_recv()

    def g_arrived(slot):
        g_send(slot, send_sem.at[0], near).wait_recv()

    docs, rels, ranks = [], [], []
    for o in range(2):
        local = 2 * j + slot_of(o)
        doc = img_ref[2 * base + local]
        rank = jnp.int32(0)
        for i in range(2 * GROUP):
            same = (img_ref[2 * base + i] == doc) & (i < local)
            rank = rank + jnp.where(same, 1, 0)
        doc = doc - base
        rel = jnp.where(
            doc == j, 0, jnp.where(doc == near - base, 1, jnp.where(doc == GROUP - 1 - j, 2, 3))
        )
        docs.append(doc)
        rels.append(rel)
        ranks.append(rank)
    gate = jnp.tanh(jnp.broadcast_to(gate_ref[...], (1, DIM)))

    @pl.when(outer)
    def _():
        for r in (2, 3):
            qbuf[r] = jnp.zeros((TEXT, HEADS * DIM), BF16)
            gbuf[r] = jnp.zeros((TEXT, HEADS * DIM), BF16)


    loads[0].wait()
    seen = []
    rank_at = lax.broadcasted_iota(jnp.int32, tm_ref.shape, 0)
    doc_at = lax.broadcasted_iota(jnp.int32, tm_ref.shape, 1)
    for o in range(2):
        hit = (rank_at == ranks[o]) & (doc_at == docs[o] + (base - base8))
        row = jnp.sum(jnp.where(hit, tm_ref[...], 0).astype(F32), axis=0)
        seen.append(jnp.sum(row, axis=0, keepdims=True))

    tail_row = lax.broadcasted_iota(jnp.int32, (PADDED - MAIN, DIM), 0) == 0

    def unit_of(x):
        inverse = lax.rsqrt(jnp.mean(x * x, axis=1, keepdims=True) + EPSILON)
        return x * inverse, inverse

    def rows_of(o, k, a, n):
        return pl.ds(4 * a + 2 * k + slot_of(o), n, stride=4)

    def tail_of(ref, o, k):
        row = ref[pl.ds(4 * MAIN + 2 * k + slot_of(o), 1), :]
        return jnp.where(tail_row, jnp.broadcast_to(row, (PADDED - MAIN, DIM)), 0.0)

    def widen(raw, wide):
        rows = raw.reshape(4 * COLS, DIM)

        def body(i, carry):
            at = pl.ds(pl.multiple_of(i * 320, 320), 320)
            wide[at, :] = rows[at, :].astype(F32)
            return carry

        lax.fori_loop(0, 4 * MAIN // 320, body, 0)
        wide[4 * MAIN : 4 * COLS, :] = rows[4 * MAIN : 4 * COLS, :].astype(F32)

    def narrow(wide, raw):
        rows = raw.reshape(4 * COLS, DIM)

        def body(i, carry):
            at = pl.ds(pl.multiple_of(i * 320, 320), 320)
            rows[at, :] = wide[at, :].astype(BF16)
            return carry

        lax.fori_loop(0, 4 * MAIN // 320, body, 0)
        rows[4 * MAIN : 4 * COLS, :] = wide[4 * MAIN : 4 * COLS, :].astype(BF16)

    loads[3].wait()
    widen(kraw, wide_k)

    q_near[1].start()
    start_where(inner, q_far[1])
    loads[4].wait()
    widen(vraw, wide_v)

    def prep_kv(u, carry):
        o, k = u // KV, u % KV
        for a in range(0, DEEP, DIM):
            if a + DIM < MAIN:
                x = wide_k[rows_of(o, k, a, DIM), :]
                v = wide_v[rows_of(o, k, a, DIM), :]
                n = DIM
            else:
                n = PADDED - a
                fill = jnp.zeros((DIM - n, DIM), F32)
                x = [wide_k[rows_of(o, k, a, MAIN - a), :], tail_of(wide_k, o, k), fill]
                v = [wide_v[rows_of(o, k, a, MAIN - a), :], tail_of(wide_v, o, k), fill]
                x, v = jnp.concatenate(x, axis=0), jnp.concatenate(v, axis=0)
            unit, _ = unit_of(x)
            hat = unit * kgain_ref[...]
            khat[o, k, a : a + n, :] = hat.astype(BF16)[:n]
            vpad[o, k, a : a + n, :] = v.astype(BF16)[:n]
            turned_k[o, k, :, a : a + DIM] = hat.T.astype(BF16)
            turned_v[o, k, :, a : a + DIM] = v.T.astype(BF16)
        return carry

    lax.fori_loop(0, 2 * KV, prep_kv, 0)

    start_where(outer, q_far[0])
    g_near.start()

    def chosen(buf, o, count, lanes):
        x = buf[0, :, lanes].astype(F32)
        for r in range(1, count):
            x = jnp.where(rels[o] == r, buf[r, :, lanes].astype(F32), x)
        return x

    def prep_q(o, k, count):
        def body(c, carry):
            hc = k * (PER // 2) + c
            x = chosen(qbuf, o, count, pl.ds(pl.multiple_of(hc * ROWS, ROWS), ROWS))
            for h in range(2):
                unit, _ = unit_of(x[:, h * DIM : (h + 1) * DIM])
                hat = unit * qgain_ref[...]
                at = pl.ds(pl.multiple_of(c * ROWS + h * TEXT, TEXT), TEXT)
                qh[o, k, at, :] = hat.astype(BF16)
                qhT[o, k, :, at] = hat.T.astype(BF16)
            return carry

        lax.fori_loop(0, PER // 2, body, 0, unroll=2)

    def put_rows(ref, o, k, row):
        for h in range(PER):
            ref[o, k * PER + h : k * PER + h + 1, :] = row[:, h * TEXT : (h + 1) * TEXT]

    def get_rows(ref, o, k):
        rows = ref[o, pl.ds(pl.multiple_of(k * PER, PER), PER), :]
        return jnp.concatenate([rows[h : h + 1] for h in range(PER)], axis=1)

    tail_mask = lax.broadcasted_iota(jnp.int32, (PADDED - MAIN, SPAN), 0) == 0
    STEP = 400

    def score_step(u, at, n, top):
        o, k = u // KV, u % KV
        s = dot(khat[o, k, at, :], qhT[o, k])
        if n < STEP:
            s = jnp.where(tail_mask, s, -jnp.inf)
        e_ref[u, at, :] = s
        return jnp.maximum(top, fold(s, jnp.max))

    def exp_step(u, at, top, total):
        e = jnp.exp2((e_ref[u, at, :] - top) * (SCALE * LOG2E))
        e_ref[u, at, :] = e
        return total + fold(e, jnp.sum)

    lowest = jnp.full((8, SPAN), -jnp.inf, F32)
    nothing = jnp.zeros((8, SPAN), F32)

    def sweep(now, ahead, top):
        def body(i, carry):
            total, high = carry
            at = pl.ds(pl.multiple_of(i * STEP, STEP), STEP)
            if ahead is not None:
                high = score_step(ahead, at, STEP, high)
            if now is not None:
                total = exp_step(now, at, top, total)
            return total, high

        total, high = lax.fori_loop(0, MAIN // STEP, body, (nothing, lowest))
        at = slice(MAIN, PADDED)
        if ahead is not None:
            high = score_step(ahead, at, PADDED - MAIN, high)
        if now is not None:
            total = exp_step(now, at, top, total)
        return jnp.sum(total, axis=0, keepdims=True), jnp.max(high, axis=0, keepdims=True)

    def weigh(u, top, total):
        o, k = u // KV, u % KV
        inverse = 1.0 / total
        out = None
        for a in range(0, PADDED, 2 * DIM):
            n = min(2 * DIM, PADDED - a)
            p = (e_ref[u, a : a + n, :] * inverse).astype(BF16)
            if n < 2 * DIM:
                p = jnp.concatenate([p, jnp.zeros((DEEP - a - n, SPAN), BF16)], axis=0)
            part = dot(turned_v[o, k, :, a : a + p.shape[0]], p)
            out = part if out is None else out + part
        o_ref[o, k] = out
        put_rows(m_ref, o, k, top * SCALE)
        put_rows(w_ref, o, k, top * SCALE + jnp.log(total))

    def ready_q(o, k):
        if o == 0:
            q_arrived(1, k)

        @pl.when(inner)
        def _():
            q_arrived(2 + o, k)

        prep_q(o, k, 3 + o)

    loads[1].wait()
    ready_q(0, 0)
    _, top = sweep(None, 0, None)
    start_where(outer, q_far[1])
    ready_q(0, 1)

    g_far.start()

    for u in range(2 * KV):
        total, ahead = sweep(u, u + 1 if u + 1 < 2 * KV else None, top)
        weigh(u, top, total)
        top = ahead
        if u + 2 < 2 * KV:
            ready_q((u + 2) // KV, (u + 2) % KV)
    loads[2].wait()
    g_arrived(1)

    @pl.when(inner)
    def _():
        g_arrived(2)
        g_arrived(3)

    for o in range(2):

        def delta(hc, carry):
            x = chosen(gbuf, o, 3 + o, pl.ds(pl.multiple_of(hc * ROWS, ROWS), ROWS))
            k, c = hc // (PER // 2), hc % (PER // 2)
            out = o_ref[o, k, :, pl.ds(pl.multiple_of(c * ROWS, ROWS), ROWS)]
            for h in range(2):
                part = slice(h * TEXT, (h + 1) * TEXT)
                put = pl.ds(pl.multiple_of(c * ROWS + h * TEXT, TEXT), TEXT)
                raw = x[:, part]
                turned_raw = raw.T
                grad = (gate * turned_raw).astype(BF16)
                gs[o, k, put, :] = (gate * raw).astype(BF16)
                gsT[o, k, :, put] = grad
                at = pl.ds(2 * hc + h, 1)
                d_ref[o, at, :] = jnp.sum(out[:, part] * grad.astype(F32), axis=0, keepdims=True)
                gam_ref[o, at, :] = jnp.sum(out[:, part] * turned_raw, axis=0, keepdims=True)
            return carry

        lax.fori_loop(0, CHUNKS, delta, 0, unroll=2)
        saw = jnp.broadcast_to(seen[o], (HEADS, TEXT)) > 0.0
        stats[j, slot_of(o), 0] = jnp.where(saw, w_ref[o], NEGATIVE)
        stats[j, slot_of(o), 1] = jnp.where(saw, d_ref[o], 0.0)

    swaps = []
    for step in range(1, GROUP):
        swaps.append(
            remote(
                stats.at[j], stats.at[j], stat_send.at[step - 1], stat_recv.at[j],
                base + (j + step) % GROUP,
            )
        )
    for c in swaps:
        c.start()

    saws = [jnp.broadcast_to(seen[o], (HEADS, TEXT)) > 0.0 for o in range(2)]
    mine_lse = [jnp.where(saws[o], w_ref[o], NEGATIVE) for o in range(2)]
    peak = jnp.maximum(mine_lse[0], mine_lse[1])
    shares = [jnp.exp(x - peak) for x in mine_lse]
    for o in range(2):
        local = jnp.where(rels[0] == rels[1], shares[o] / (shares[0] + shares[1]), 1.0)
        lw_ref[o] = jnp.where(saws[o], local, 0.0)

    def total_of(pair, r):
        a = jnp.where(rels[0] == r, pair[0], 0.0)
        return a + jnp.where(rels[1] == r, pair[1], 0.0)

    def share_far(pair, far_b, k, lanes):
        far_b[0, k, :, lanes] = total_of(pair, 2).astype(BF16)
        far_b[1, k, :, lanes] = total_of(pair, 3).astype(BF16)

    def share_near(pair, own_b, near_b, k, lanes):
        own_b[k, :, lanes] = total_of(pair, 0)
        near_b[k, :, lanes] = total_of(pair, 1)

    def returns(which, k, near_b, far_b, rnear_b, rfar_b):
        one = remote(
            near_b.at[k], rnear_b.at[k], ret_send.at[which, k, 0], ret_recv.at[which, k, 0], near
        )
        two = [
            remote(
                far_b.at[r, k], rfar_b.at[k], ret_send.at[which, k, 1 + r],
                ret_recv.at[which, k, 1], base + jnp.where(j == 1, 2 + r, 1 - r),
            )
            for r in range(2)
        ]
        return one, two

    def start_far(*args):
        start_where(inner, *returns(*args)[1])

    def start_near(*args):
        returns(*args)[0].start()

    def finish_sends(*args):
        one, two = returns(*args)
        one.wait_send()

        @pl.when(inner)
        def _():
            for c in two:
                c.wait_send()

    def wait_returns(*args):
        one, two = returns(*args)
        one.wait_recv()
        two[0].wait_recv()

    o_args = (near_o, far_o, rnear_o, rfar_o)
    q_args = (near_q, far_q, rnear_q, rfar_q)

    def give_out(k, carry):
        def body(c, carry):
            hc = k * (PER // 2) + c
            pair = []
            for o in range(2):
                w = [lw_ref[o, pl.ds(2 * hc + h, 1), :] for h in range(2)]
                x = o_ref[o, k, :, pl.ds(pl.multiple_of(c * ROWS, ROWS), ROWS)]
                x = x * jnp.concatenate(w, axis=1)
                pair.append(jnp.concatenate([x[:, :TEXT].T, x[:, TEXT:].T], axis=1))
            lanes = pl.ds(pl.multiple_of(c * ROWS, ROWS), ROWS)
            share_far(pair, far_o, k, lanes)
            share_near(pair, own_o, near_o, k, lanes)
            return carry

        lax.fori_loop(0, PER // 2, body, 0, unroll=2)
        start_far(0, k, *o_args)
        start_near(0, k, *o_args)
        return carry

    lax.fori_loop(0, KV, give_out, 0)

    for step in range(1, GROUP):
        other = (j + step) % GROUP
        remote(stats.at[j], stats.at[other], stat_send.at[0], stat_recv.at[other], near).wait_recv()

    def of_document(doc):
        mine = [img_ref[2 * base + i] - base == doc for i in range(2 * GROUP)]
        lses = [
            jnp.where(mine[i], stats[i // 2, i % 2, 0], 2.0 * NEGATIVE) for i in range(2 * GROUP)
        ]
        top = functools.reduce(jnp.maximum, lses)
        terms = [jnp.exp(x - top) for x in lses]
        return mine, top, terms, functools.reduce(jnp.add, terms)

    _, _, terms, total = of_document(j)
    for r, holder in enumerate((j, near - base, far - base)):
        weight = jnp.zeros((HEADS, TEXT), F32)
        for i in range(2 * GROUP):
            weight = weight + jnp.where(holder == i // 2, terms[i], 0.0)
        fill = jnp.zeros((DIM - HEADS, TEXT), F32)
        wt_ref[r] = jnp.concatenate([weight / total, fill], axis=0).T

    gate_sum = jnp.zeros((HEADS, TEXT), F32)
    for o in range(2):
        mine, top, terms, total = of_document(docs[o])
        weighted = [
            t * jnp.where(mine[i], stats[i // 2, i % 2, 1], 0.0) for i, t in enumerate(terms)
        ]
        saw = jnp.broadcast_to(seen[o], (HEADS, TEXT)) > 0.0
        own = jnp.where(saw, w_ref[o], NEGATIVE)
        d_ref[o] = functools.reduce(jnp.add, weighted) / total
        f_ref[o] = jnp.where(saw, jnp.exp(m_ref[o] - (top + jnp.log(total))), 0.0)
        w_ref[o] = jnp.where(saw, jnp.exp(own - top) / total, 0.0)
        gate_sum = gate_sum + w_ref[o] * gam_ref[o]

    def backward(k, sums):
        kgain_sum, qgain_sum = sums

        def per_slot(o, carry):
            factor = get_rows(f_ref, o, k)
            delta = get_rows(d_ref, o, k)
            for a in range(0, PADDED, 2 * DIM):
                n = min(2 * DIM, PADDED - a)
                dp = dot(vpad[o, k, a : a + n, :], gsT[o, k])
                p = e_ref[2 * o + k, a : a + n, :] * factor
                ds = (p * (dp - delta)).astype(BF16)
                value = crossed(gsT[o, k], p.astype(BF16)).T
                e_ref[2 * o + k, a : a + n, :DIM] = crossed(qhT[o, k], ds).T
                if n < 2 * DIM:
                    ds = jnp.concatenate([ds, jnp.zeros((DEEP - a - n, SPAN), BF16)], axis=0)
                part = dot(turned_k[o, k, :, a : a + ds.shape[0]], ds)
                if a == 0:
                    x_acc[...] = part
                else:
                    x_acc[...] += part
                whole = min(n, MAIN - a)
                wide_v[rows_of(o, k, a, whole), :] = value[:whole]
                if whole < n:
                    wide_v[pl.ds(4 * MAIN + 2 * k + slot_of(o), 1), :] = value[whole : whole + 1]
            for c in range(PER // 2):
                dq_ref[o, c] = jnp.concatenate(
                    [x_acc[:, c * ROWS + h * TEXT : c * ROWS + (h + 1) * TEXT].T for h in range(2)], axis=1
                )
            return carry

        lax.fori_loop(0, 2, per_slot, 0)

        def give_far(c, carry):
            lanes = pl.ds(pl.multiple_of(c * ROWS, ROWS), ROWS)
            share_far([dq_ref[0, c], dq_ref[1, c]], far_q, k, lanes)
            return carry

        lax.fori_loop(0, PER // 2, give_far, 0, unroll=2)
        start_far(1, k, *q_args)

        def body(c, qgain_sum):
            pair = [dq_ref[0, c], dq_ref[1, c]]
            share_near(pair, own_q, near_q, k, pl.ds(pl.multiple_of(c * ROWS, ROWS), ROWS))
            full = pl.ds(pl.multiple_of(k * PER * DIM + c * ROWS, ROWS), ROWS)
            for o in range(2):
                x = chosen(qbuf, o, 3 + o, full)
                for h in range(2):
                    part = slice(h * DIM, (h + 1) * DIM)
                    unit, _ = unit_of(x[:, part])
                    qgain_sum = qgain_sum + fold(pair[o][:, part] * unit, jnp.sum)
            return qgain_sum

        qgain_sum = lax.fori_loop(0, PER // 2, body, qgain_sum, unroll=2)
        start_near(1, k, *q_args)

        def norm_back(o, kgain_sum):
            def key_step(x, up, kgain_sum):
                up = up * SCALE
                unit, inverse = unit_of(x)
                scaled = up * kgain_ref[...]
                back = inverse * (scaled - unit * jnp.mean(scaled * unit, axis=1, keepdims=True))
                return back, kgain_sum + fold(up * unit, jnp.sum)

            for a in range(0, MAIN, STEP):
                at = rows_of(o, k, a, STEP)
                back, kgain_sum = key_step(wide_k[at, :], e_ref[2 * o + k, a : a + STEP, :DIM], kgain_sum)
                wide_k[at, :] = back
            back, kgain_sum = key_step(
                tail_of(wide_k, o, k), e_ref[2 * o + k, MAIN:PADDED, :DIM], kgain_sum
            )
            wide_k[pl.ds(4 * MAIN + 2 * k + slot_of(o), 1), :] = back[:1]
            return kgain_sum

        return lax.fori_loop(0, 2, norm_back, kgain_sum), qgain_sum

    zero = jnp.zeros((8, DIM), F32)
    kgain_sum, qgain_sum = lax.fori_loop(0, KV, backward, (zero, zero))

    row = lax.broadcasted_iota(jnp.int32, (8, DIM), 0)
    gate_total = jnp.sum(jnp.sum(gate_sum, axis=0, keepdims=True), axis=1, keepdims=True)
    part = jnp.where(
        row == 0,
        jnp.sum(qgain_sum, axis=0, keepdims=True) * SCALE,
        jnp.where(
            row == 1,
            jnp.sum(kgain_sum, axis=0, keepdims=True),
            (1.0 - gate * gate) * gate_total,
        ),
    )

    def stage_copies(n):
        axis, stride, count, mine, low = place(stages[n])
        buf = sum_bufs[n]
        out, come = [], []
        for step in range(1, count):
            other = (mine + step) % count
            for at, to, found in ((mine, out, step), (other, come, 0)):
                to.append(
                    pltpu.make_async_remote_copy(
                        src_ref=buf.at[at], dst_ref=buf.at[at], send_sem=sum_send.at[n, found],
                        recv_sem=sum_recv.at[n, at], device_id={axis: low + stride * other},
                        device_id_type=MESH,
                    )
                )
        return out, come

    def stage_start(n, value):
        sum_bufs[n][place(stages[n])[3]] = value
        for c in stage_copies(n)[0]:
            c.start()

    def stage_end(n):
        for c in stage_copies(n)[1]:
            c.wait_recv()
        value = sum_bufs[n][0]
        for i in range(1, stages[n][2]):
            value = value + sum_bufs[n][i]
        return value

    stage_start(0, part)

    outs = [
        pltpu.make_async_copy(kraw, dk_hbm, out_sem.at[0]),
        pltpu.make_async_copy(vraw, dv_hbm, out_sem.at[1]),
    ]
    narrow(wide_k, kraw)
    outs[0].start()
    narrow(wide_v, vraw)
    outs[1].start()
    part = stage_end(0)
    if len(stages) > 1:
        stage_start(1, part)

    for k in range(KV):
        wait_returns(0, k, *o_args)

    for h in range(HEADS):
        k, lanes = h // PER, slice(h % PER * DIM, (h % PER + 1) * DIM)
        parts = (own_o[k, :, lanes], rnear_o[k, :, lanes], rfar_o[k, :, lanes].astype(F32))
        merged = functools.reduce(
            jnp.add, [wt_ref[r, :, h : h + 1] * x for r, x in enumerate(parts)]
        )
        gbuf[0, :, h * DIM : (h + 1) * DIM] = (gate * merged).astype(BF16)
    out_att = pltpu.make_async_copy(gbuf.at[0], att_hbm.at[0], out_sem.at[4])
    out_att.start()
    if len(stages) > 1:
        part = stage_end(1)
    if len(stages) > 2:
        stage_start(2, part)

    for k in range(KV):
        wait_returns(1, k, *q_args)

    def finish(k, carry):
        for c in range(PER):
            lanes = slice(c * DIM, (c + 1) * DIM)
            full = pl.ds(pl.multiple_of(k * PER * DIM + c * DIM, DIM), DIM)
            hat = own_q[k, :, lanes] + rnear_q[k, :, lanes] + rfar_q[k, :, lanes].astype(F32)
            hat = hat * SCALE
            unit, inverse = unit_of(qbuf[0, :, full].astype(F32))
            scaled = hat * qgain_ref[...]
            back = inverse * (scaled - unit * jnp.mean(scaled * unit, axis=1, keepdims=True))
            qbuf[0, :, full] = back.astype(BF16)
        return carry

    lax.fori_loop(0, KV, finish, 0)
    out_dq = pltpu.make_async_copy(qbuf.at[0], dq_hbm.at[0], out_sem.at[5])
    out_dq.start()

    if len(stages) > 2:
        part = stage_end(2)
    qg_out[...] = part[0:1]
    kg_out[...] = part[1:2]
    gate_out[...] = part[2:3, 0:1]
    for n in range(len(stages)):
        for c in stage_copies(n)[0]:
            c.wait_send()
    for c in (*q_near, *q_far, g_near, g_far):
        c.wait_send()
    for c in swaps:
        c.wait_send()
    for k in range(KV):
        finish_sends(0, k, *o_args)
        finish_sends(1, k, *q_args)
    for c in outs:
        c.wait()
    out_att.wait()
    out_dq.wait()


def run_main(stages, img, gate, qgain, kgain, text_mask, q, g, kk, vv):
    vm = pltpu.VMEM
    dma = pltpu.SemaphoreType.DMA
    half = (KV, TEXT, PER * DIM)
    slots = text_mask.shape[0]
    scratch = [
        vm((slots, 8, TEXT), jnp.int32),
        vm((4, TEXT, HEADS * DIM), BF16),
        vm((4, TEXT, HEADS * DIM), BF16),
        vm((COLS, 4, DIM), BF16),
        vm((COLS, 4, DIM), BF16),
        vm((4 * PADDED, DIM), F32),
        vm((4 * PADDED, DIM), F32),
        vm((2, KV, PADDED, DIM), BF16),
        vm((2, KV, PADDED, DIM), BF16),
        vm((2, KV, DIM, DEEP), BF16),
        vm((2, KV, DIM, DEEP), BF16),
        vm((2, KV, SPAN, DIM), BF16),
        vm((2, KV, DIM, SPAN), BF16),
        vm((2, KV, SPAN, DIM), BF16),
        vm((2, KV, DIM, SPAN), BF16),
        vm((2 * KV, PADDED, SPAN), F32),
        vm((2, KV, DIM, SPAN), F32),
        vm((2, PER // 2, TEXT, ROWS), F32),
        vm((DIM, SPAN), F32),
        vm((2, HEADS, TEXT), F32),
        vm((2, HEADS, TEXT), F32),
        vm((2, HEADS, TEXT), F32),
        vm((2, HEADS, TEXT), F32),
        vm((2, HEADS, TEXT), F32),
        vm((2, HEADS, TEXT), F32),
        vm((3, TEXT, DIM), F32),
        vm((GROUP, 2, 2, HEADS, TEXT), F32),
        vm(half, F32),
        vm(half, F32),
        vm((2,) + half, BF16),
        vm(half, F32),
        vm(half, F32),
        vm((2,) + half, BF16),
        vm(half, F32),
        vm(half, BF16),
        vm(half, F32),
        vm(half, BF16),
        dma((7,)),
        dma((6,)),
        dma((3, 4)),
        dma((3,)),
        dma((4,)),
        dma((2, KV, 3)),
        dma((2, KV, 2)),
        dma((6,)),
        dma((len(stages), max(s[2] for s in stages))),
        dma((len(stages), max(s[2] for s in stages))),
    ] + [vm((s[2], 8, DIM), F32) for s in stages]
    hbm = pl.BlockSpec(memory_space=pl.ANY)
    vmem = pl.BlockSpec(memory_space=pltpu.VMEM)
    return pl.pallas_call(
        functools.partial(main_kernel, stages),
        out_shape=(
            jax.ShapeDtypeStruct(q.shape, BF16),
            jax.ShapeDtypeStruct(q.shape, BF16),
            jax.ShapeDtypeStruct(kk.shape, BF16),
            jax.ShapeDtypeStruct(vv.shape, BF16),
            jax.ShapeDtypeStruct((1, DIM), F32),
            jax.ShapeDtypeStruct((1, DIM), F32),
            jax.ShapeDtypeStruct((1, 1), F32),
        ),
        in_specs=[pl.BlockSpec(memory_space=pltpu.SMEM), vmem, vmem, vmem] + [hbm] * 5,
        out_specs=(hbm, hbm, hbm, hbm, vmem, vmem, vmem),
        scratch_shapes=scratch,
        compiler_params=pltpu.CompilerParams(
            collective_id=0, has_side_effects=True, vmem_limit_bytes=64 * 1024 * 1024
        ),
    )(img, gate, qgain, kgain, text_mask, q, g, kk, vv)


def stages_of(sizes):
    low = min(8, sizes["dp"])
    out = [("dp", 1, low)]
    if sizes["heads"] > 1:
        out.append(("heads", 1, sizes["heads"]))
    if sizes["dp"] > low:
        out.append(("dp", low, sizes["dp"] // low))
    return out


PIECES = 4


def copy_kernel(count, *refs):
    stage = refs[2 * count : 3 * count]
    come, leave = refs[3 * count :]
    pairs = []
    for i in range(count):
        rows = refs[i].shape[0]
        size = -(-rows // PIECES)
        for n, a in enumerate(range(0, rows, size)):
            at = pl.ds(a, min(size, rows - a))
            pairs.append(
                (
                    pltpu.make_async_copy(refs[i].at[at], stage[i].at[at], come.at[i, n]),
                    pltpu.make_async_copy(stage[i].at[at], refs[count + i].at[at], leave.at[i, n]),
                )
            )
    for first, _ in pairs:
        first.start()
    for first, second in pairs:
        first.wait()
        second.start()
    for _, second in pairs:
        second.wait()


def settled(*arrays):
    hbm = pl.BlockSpec(memory_space=pl.ANY)
    count = len(arrays)
    return pl.pallas_call(
        functools.partial(copy_kernel, count),
        out_shape=tuple(jax.ShapeDtypeStruct(a.shape, a.dtype) for a in arrays),
        in_specs=[hbm] * count,
        out_specs=(hbm,) * count,
        scratch_shapes=[pltpu.VMEM(a.shape, a.dtype) for a in arrays]
        + [pltpu.SemaphoreType.DMA((count, PIECES))] * 2,
        compiler_params=pltpu.CompilerParams(vmem_limit_bytes=64 * 1024 * 1024),
    )(*arrays)


def interleaved(x):
    x = x.transpose(1, 0, 2).reshape(COLS, 2, KV, DIM)
    return x.transpose(0, 2, 1, 3).reshape(COLS, 2 * KV, DIM)


def separated(x):
    return x.reshape(COLS, KV, 2, DIM).transpose(2, 0, 1, 3).reshape(2, COLS, KV * DIM)


def solution(mesh):
    sizes = dict(mesh.shape)

    def per_device(q, qgain, kk, vv, kgain, gate, img, text_mask, g):
        found = run_main(
            stages_of(sizes), img, gate.reshape(1, 1), qgain.reshape(1, DIM),
            kgain.reshape(1, DIM), text_mask.transpose(2, 0, 1), q, g, interleaved(kk),
            interleaved(vv),
        )
        att, dq, dk, dv, qg, kg, gt = settled(*found)
        return (
            att, dq, separated(dk), separated(dv), qg.reshape(DIM), kg.reshape(DIM), gt.reshape(1)
        )

    split = P("dp", None, "heads")
    return jax.shard_map(
        per_device,
        mesh=mesh,
        in_specs=(split, P(), split, split, P(), P(), P(), P(), split),
        out_specs=(split, split, split, split, P(), P(), P()),
        check_vma=False,
    )
```
